128 devices in a mesh: fsdp: 16 (over z, y_lo, core), tp: 8 (over y_hi, x).
Axes of the slice: x: 4, y: 4 (y_hi: 2, y_lo: 2; y = y_hi * 2 + y_lo), z: 4, core: 2. Of those that a mesh axis runs over, the one named last changes fastest.
Arguments:
- block_input: bfloat16 [16384, 2048], P(('fsdp', 'tp')), may hold values from -6 to 6
- norm_gain: bfloat16 [2048], P('fsdp'), may hold values from 0.099609375 to 1.8984375
- norm_bias: bfloat16 [2048], P('fsdp'), may hold values from -3 to 3
- qkv_weight: bfloat16 [2048, 3, 2048], P('fsdp', None, 'tp'), may hold values from -0.125 to 0.125
- qkv_bias: bfloat16 [3, 2048], P(None, 'tp'), may hold values from -3 to 3
- dense_weight: bfloat16 [2048, 2048], P('tp', 'fsdp'), may hold values from -1 to 1
- dense_bias: bfloat16 [2048], P('fsdp'), may hold values from -3 to 3
- up_weight: bfloat16 [2048, 8192], P('fsdp', 'tp'), may hold values from -0.125 to 0.125
- up_bias: bfloat16 [8192], P('tp'), may hold values from -3 to 3
- down_weight: bfloat16 [8192, 2048], P('tp', 'fsdp'), may hold values from -0.0625 to 0.0625
- down_bias: bfloat16 [2048], P('fsdp'), may hold values from -3 to 3
- cotangent: bfloat16 [16384, 2048], P(('fsdp', 'tp')), may hold values from -6 to 6
Outputs:
- block_output: bfloat16 [16384, 2048], P(('fsdp', 'tp'))
- input_grad: bfloat16 [16384, 2048], P(('fsdp', 'tp'))
- grad_norm_gain: float32 [2048], P('fsdp')
- grad_norm_bias: float32 [2048], P('fsdp')
- grad_qkv_weight: float32 [2048, 3, 2048], P('fsdp', None, 'tp')
- grad_qkv_bias: float32 [3, 2048], P(None, 'tp')
- grad_dense_weight: float32 [2048, 2048], P('tp', 'fsdp')
- grad_dense_bias: float32 [2048], P('fsdp')
- grad_up_weight: float32 [2048, 8192], P('fsdp', 'tp')
- grad_up_bias: float32 [8192], P('tp')
- grad_down_weight: float32 [8192, 2048], P('tp', 'fsdp')
- grad_down_bias: float32 [2048], P('fsdp')
The draws below stay inside these ranges and needn't reach their ends.
All inputs are finite; a program needn't handle non-finite values.
Results may differ from the reference program's by a relative error of at most 0.02.
Values may be sent and summed in bfloat16 or wider, within the bound.
A program may use at most 128 MiB of HBM per device.

```python
import jax
import jax.numpy as jnp
from jax import lax

D = 2048
H = 32
HD = 64
ROT = 32
FF = 8192
SEQ_LEN = 1024
TOKENS = 16384


def steps_of(own_key, shape, pieces, smallest, largest):
    def one(axis_at, blocks):
        heights = jax.random.uniform(jax.random.fold_in(jax.random.fold_in(own_key, 6), axis_at), (blocks,), jnp.float32, smallest / len(pieces), largest / len(pieces))
        return jnp.repeat(jnp.exp(heights), shape[axis_at] // blocks).reshape((-1,) + (1,) * (len(shape) - axis_at - 1))

    gain = one(*pieces[0])
    for cut in pieces[1:]:
        gain = gain * one(*cut)
    return gain


def bell_draw(rng, shape, deviation, reach, shards=(), kind=jnp.bfloat16):
    gain = steps_of(rng, shape, shards, -0.22, 0.18) if shards else 1.0
    drawn = jax.random.normal(rng, shape, jnp.float32) * deviation * gain
    return jnp.minimum(jnp.maximum(drawn, -reach), reach).astype(kind)


def setup_inputs(seed: int = 0) -> dict:
    key_list = jax.random.split(jax.random.key(seed), 13)
    block_input = bell_draw(key_list[0], (TOKENS, D), 1.0, 6.0, ((0, 128),))
    norm_gain = jnp.clip(1.0 + 0.18 * jax.random.normal(key_list[1], (D,), jnp.float32), 0.099609375, 1.8984375).astype(jnp.bfloat16)
    norm_bias = bell_draw(key_list[2], (D,), 0.3, 3.0, ((0, 16),))
    qkv_weight = bell_draw(key_list[3], (D, 3, H * HD), D ** -0.5, 0.125, ((0, 16), (2, 8)))
    qkv_bias = bell_draw(key_list[4], (3, H * HD), 0.5, 3.0, ((1, 8),))
    dense_weight = bell_draw(key_list[5], (H * HD, D), (max(D // 64, 4)) ** -0.5, 1.0, ((0, 8), (1, 16)))
    dense_bias = bell_draw(key_list[6], (D,), 0.5, 3.0, ((0, 16),))
    up_weight = bell_draw(key_list[7], (D, FF), D ** -0.5, 0.125, ((0, 16), (1, 8)))
    up_bias = bell_draw(key_list[8], (FF,), 0.5, 3.0, ((0, 8),))
    down_weight = bell_draw(key_list[9], (FF, D), FF ** -0.5, 0.0625, ((0, 8), (1, 16)))
    down_bias = bell_draw(key_list[10], (D,), 0.5, 3.0, ((0, 16),))
    cotangent = bell_draw(key_list[11], (TOKENS, D), 1.0, 6.0, ((0, 128),))
    return dict(block_input=block_input, norm_gain=norm_gain, norm_bias=norm_bias, qkv_weight=qkv_weight, qkv_bias=qkv_bias, dense_weight=dense_weight, dense_bias=dense_bias, up_weight=up_weight, up_bias=up_bias, down_weight=down_weight, down_bias=down_bias, cotangent=cotangent)


EPS = 1e-05

@jax.custom_vjp
def low(v):
    return lax.optimization_barrier(v.astype(jnp.bfloat16)).astype(jnp.float32)

@jax.custom_vjp
def low_back(v):
    return v

def low_keep(v):
    return (low(v), None)

def low_pass(kept, grad):
    return (grad,)

def back_keep(v):
    return (v, None)

def back_low(kept, grad):
    return (low(grad),)
low.defvjp(low_keep, low_pass)
low_back.defvjp(back_keep, back_low)

def rotary_tables():
    positions = jnp.arange(SEQ_LEN, dtype=jnp.float32)
    freqs = 10000.0 ** (-jnp.arange(ROT // 2, dtype=jnp.float32) * 2.0 / ROT)
    angles = positions[:, None] * freqs[None, :]
    return (jnp.cos(angles)[:, None, :], jnp.sin(angles)[:, None, :])

def rotate(values, cos_table, sin_table):
    half_rot = ROT // 2
    first_half = values[..., :half_rot]
    second = values[..., half_rot:ROT]
    return jnp.concatenate([first_half * cos_table - second * sin_table, second * cos_table + first_half * sin_table, values[..., ROT:]], axis=-1)

def forward(input_rows, norm_gain, norm_bias, qkv_weight, qkv_bias, dense_weight, dense_bias, up_weight, up_bias, down_weight, down_bias):
    highest = lax.Precision.HIGHEST
    row_mean = lax.optimization_barrier(jnp.mean(input_rows, axis=-1, keepdims=True))
    centered = input_rows - row_mean
    variance = lax.optimization_barrier(jnp.mean(centered * centered, axis=-1, keepdims=True))
    normed = low(centered * lax.rsqrt(variance + EPS) * norm_gain + norm_bias)
    inner_width = H * HD
    joined_qkv = jnp.dot(normed, qkv_weight.reshape(D, 3 * inner_width), precision=highest) + qkv_bias.reshape(3 * inner_width)
    joined_qkv = low_back(joined_qkv).reshape(SEQ_LEN, 3, H, HD)
    cos_table, sin_table = rotary_tables()
    queries = low(rotate(joined_qkv[:, 0], cos_table, sin_table))
    rotated_keys = low(rotate(joined_qkv[:, 1], cos_table, sin_table))
    values = low(joined_qkv[:, 2])
    score_scale = HD ** (-0.5)
    scores = low_back(jnp.einsum('qhd,khd->hqk', queries, rotated_keys, precision=highest) * score_scale)
    causal = jnp.arange(SEQ_LEN)[None, :] <= jnp.arange(SEQ_LEN)[:, None]
    scores = jnp.where(causal[None], scores, -1e+30)
    weights = low(jax.nn.softmax(scores, axis=-1))
    context = jnp.einsum('hqk,khd->qhd', weights, values, precision=highest).reshape(SEQ_LEN, inner_width)
    context = low_back(low(context))
    attended = jnp.dot(context, dense_weight, precision=highest)
    hidden = low_back(jnp.dot(normed, up_weight, precision=highest) + up_bias)
    active = low(jax.nn.gelu(hidden, approximate=True))
    mlp_out = jnp.dot(active, down_weight, precision=highest)
    return input_rows + attended + mlp_out + dense_bias + down_bias

def reference(block_input, norm_gain, norm_bias, qkv_weight, qkv_bias, dense_weight, dense_bias, up_weight, up_bias, down_weight, down_bias, cotangent):
    params = tuple((tensor.astype(jnp.float32) for tensor in (norm_gain, norm_bias, qkv_weight, qkv_bias, dense_weight, dense_bias, up_weight, up_bias, down_weight, down_bias)))
    input_rows = block_input.astype(jnp.float32).reshape(-1, SEQ_LEN, D)
    cot_rows = cotangent.astype(jnp.float32).reshape(-1, SEQ_LEN, D)

    def one_sequence(totals, seq_pair):
        seq_rows, seq_cot = seq_pair
        result, pullback = jax.vjp(forward, seq_rows, *params)
        gradients = pullback(seq_cot)
        totals = tuple((summed + gradient for summed, gradient in zip(totals, gradients[1:])))
        return (totals, (result, gradients[0]))
    initial = tuple((jnp.zeros_like(tensor) for tensor in params))
    totals, (results, row_grads) = lax.scan(one_sequence, initial, (input_rows, cot_rows))
    return (results.reshape(-1, D).astype(jnp.bfloat16), row_grads.reshape(-1, D).astype(jnp.bfloat16), totals[0], totals[1], totals[2], totals[3], totals[4], totals[5], totals[6], totals[7], totals[8], totals[9])
```

```python
import functools

import jax
import jax.numpy as jnp
from jax import lax
from jax.experimental import pallas as pl
from jax.experimental.pallas import tpu as pltpu
from jax.sharding import PartitionSpec as P

HD = 64
ROT = 32
SEQ_LEN = 1024
EPS = 1e-05
D = 2048
TOK = 128
WA = 1792
WB = 1280
F32 = jnp.float32
BF16 = jnp.bfloat16
MESH = pl.DeviceIdType.MESH
ANY = pl.BlockSpec(memory_space=pl.ANY)
VMEM = pl.BlockSpec(memory_space=pltpu.VMEM)


def place():
    f = lax.axis_index("fsdp")
    t = lax.axis_index("tp")
    return f, t, lax.div(f, 4), lax.rem(lax.div(f, 2), 2), lax.rem(f, 2), lax.div(t, 4), lax.rem(t, 4)


def greet(peers):
    barrier = pltpu.get_barrier_semaphore()
    for peer in peers:
        pl.semaphore_signal(barrier, inc=1, device_id=peer, device_id_type=MESH)
    pl.semaphore_wait(barrier, len(peers))


def all_peers(f, t):
    peers = [(lax.rem(f + d, 16), t) for d in range(1, 16)]
    return peers + [(f, lax.rem(t + d, 8)) for d in range(1, 8)]


def remote(src, dst, ssem, rsem, to):
    return pltpu.make_async_remote_copy(
        src_ref=src, dst_ref=dst, send_sem=ssem, recv_sem=rsem, device_id=to, device_id_type=MESH
    )


class Group:
    def __init__(self, axis):
        f, t, z, yl, c, yh, x = place()
        self.axis = axis
        if axis == "tp":
            self.k, self.r, self.c = x, yh, 0
            self.dev = lambda r, k: (f, r * 4 + k)
        else:
            self.k, self.r, self.c = z, yl, c
            self.dev = lambda r, k: ((k * 2 + r) * 2 + c, t)
            self.sib = ((z * 2 + yl) * 2 + 1 - c, t)
        self.up, self.down, self.far = lax.rem(self.k + 1, 4), lax.rem(self.k + 3, 4), lax.rem(self.k + 2, 4)
        self.other = 1 - self.r

    def index(self, r, k, c=None):
        if self.axis == "tp":
            return r * 4 + k
        return (k * 2 + r) * 2 + (self.c if c is None else c)


class Gather:
    def __init__(self, group, block, half, ssem, rsem, sibling=False):
        g = self.g = group
        self.ssem, self.rsem = ssem, rsem
        self.sibling = sibling
        own = block(g.index(g.r, g.k))
        self.plan = {
            0: (own, block(g.index(g.other, g.k)), g.dev(g.other, g.k)),
            1: (own, block(g.index(g.r, g.down)), g.dev(g.r, g.up)),
            2: (own, block(g.index(g.r, g.up)), g.dev(g.r, g.down)),
            3: (block(g.index(g.other, g.k)), block(g.index(g.other, g.down)), g.dev(g.r, g.up)),
            4: (block(g.index(g.other, g.k)), block(g.index(g.other, g.up)), g.dev(g.r, g.down)),
            5: (half(g.index(g.r, g.down), 0), half(g.index(g.r, g.far), 0), g.dev(g.r, g.up)),
            6: (half(g.index(g.r, g.up), 1), half(g.index(g.r, g.far), 1), g.dev(g.r, g.down)),
            7: (half(g.index(g.other, g.down), 0), half(g.index(g.other, g.far), 0), g.dev(g.r, g.up)),
            8: (half(g.index(g.other, g.up), 1), half(g.index(g.other, g.far), 1), g.dev(g.r, g.down)),
        }
        if sibling:
            order = [(g.r, g.k), (g.other, g.k), (g.r, g.down), (g.r, g.up)]
            order += [(g.other, g.down), (g.other, g.up), (g.r, g.far), (g.other, g.far)]
            for n, (r, k) in enumerate(order):
                self.plan[9 + n] = (block(g.index(r, k)), block(g.index(r, k, 1 - g.c)), g.sib)

    def send(self, n):
        src, _, to = self.plan[n]
        remote(src, src, self.ssem.at[n], self.rsem.at[n], to).start()

    def recv(self, n):
        src, dst, to = self.plan[n]
        remote(dst, dst, self.ssem.at[n], self.rsem.at[n], to).wait_recv()

    def pass_on(self, n):
        if self.sibling:
            self.send(n)

    def start(self):
        for n in (0, 1, 2):
            self.send(n)
        self.pass_on(9)

    def pair(self):
        self.recv(0)
        self.send(3)
        self.send(4)
        self.pass_on(10)

    def near(self):
        self.recv(1)
        self.send(5)
        self.recv(2)
        self.send(6)
        self.pass_on(11)
        self.pass_on(12)

    def near_other(self):
        self.recv(3)
        self.send(7)
        self.recv(4)
        self.send(8)
        self.pass_on(13)
        self.pass_on(14)

    def far(self):
        self.recv(5)
        self.recv(6)
        self.pass_on(15)
        self.recv(7)
        self.recv(8)
        self.pass_on(16)

    def finish(self):
        if self.sibling:
            for n in range(9, 17):
                self.recv(n)
        for n, (src, _, to) in self.plan.items():
            remote(src, src, self.ssem.at[n], self.rsem.at[n], to).wait_send()


def add_rows(out, ins, chunk):
    @pl.loop(0, out.shape[0] // chunk)
    def _(i):
        rows = pl.ds(pl.multiple_of(i * chunk, chunk), chunk)
        total = ins[0][rows, :].astype(F32)
        for ref in ins[1:]:
            total = total + ref[rows, :].astype(F32)
        out[rows, :] = total.astype(out.dtype)


class Scatter:
    def __init__(self, group, block, half, far, near, pair, ssem, rsem, chunk, sib=None):
        g = self.g = group
        self.block, self.half, self.chunk = block, half, chunk
        self.far_ref, self.near_ref, self.pair_ref, self.sib_ref = far, near, pair, sib
        self.ssem, self.rsem = ssem, rsem
        self.plan = {}
        for n, r in ((0, g.other), (4, g.r)):
            slot = n // 4
            self.plan[n] = (half(g.index(r, g.far), 0), far.at[slot, 0], g.dev(g.r, g.up))
            self.plan[n + 1] = (half(g.index(r, g.far), 1), far.at[slot, 1], g.dev(g.r, g.down))
            self.plan[n + 2] = (block(g.index(r, g.up)), near.at[slot, 0], g.dev(g.r, g.up))
            self.plan[n + 3] = (block(g.index(r, g.down)), near.at[slot, 1], g.dev(g.r, g.down))
        self.plan[8] = (block(g.index(g.other, g.k)), pair, g.dev(g.other, g.k))
        if sib is not None:
            for n in range(8):
                self.plan[9 + n] = (block(n * 2 + 1 - g.c), sib.at[n], g.sib)

    def send(self, n):
        src, dst, to = self.plan[n]
        remote(src, dst, self.ssem.at[n], self.rsem.at[n], to).start()

    def recv(self, n):
        src, dst, to = self.plan[n]
        remote(src, dst, self.ssem.at[n], self.rsem.at[n], to).wait_recv()

    def sib_start(self):
        for n in range(8):
            self.send(9 + n)

    def sib_add(self):
        for n in range(8):
            self.recv(9 + n)
            mine = self.block(n * 2 + self.g.c)
            add_rows(mine, [mine, self.sib_ref.at[n]], self.chunk)

    def start(self):
        for n in (0, 1, 4, 5):
            self.send(n)

    def near(self, slot):
        g = self.g
        r = g.r if slot else g.other
        n = 4 * slot
        self.recv(n)
        mine = self.half(g.index(r, g.up), 0)
        add_rows(mine, [mine, self.far_ref.at[slot, 0]], self.chunk)
        self.send(n + 2)
        self.recv(n + 1)
        mine = self.half(g.index(r, g.down), 1)
        add_rows(mine, [mine, self.far_ref.at[slot, 1]], self.chunk)
        self.send(n + 3)

    def pair(self):
        g = self.g
        self.recv(2)
        self.recv(3)
        mine = self.block(g.index(g.other, g.k))
        add_rows(mine, [mine, self.near_ref.at[0, 0], self.near_ref.at[0, 1]], self.chunk)
        self.send(8)

    def last(self):
        g = self.g
        self.recv(6)
        self.recv(7)
        self.recv(8)
        return [self.block(g.index(g.r, g.k)), self.near_ref.at[1, 0], self.near_ref.at[1, 1], self.pair_ref]

    def finish(self):
        for n, (src, dst, to) in self.plan.items():
            remote(src, dst, self.ssem.at[n], self.rsem.at[n], to).wait_send()


def wa_half(ref):
    return lambda i, h: ref.at[i, pl.ds(h * 64, 64)]


def wb_block(ref):
    return lambda i: ref.at[:, pl.ds(pl.multiple_of(i * 128, 128), 128)]


def wb_half(ref):
    return lambda i, h: ref.at[pl.ds(h * (WB // 2), WB // 2), pl.ds(pl.multiple_of(i * 128, 128), 128)]


def token_half(ref):
    return lambda i, h: ref.at[i, pl.ds(h * (TOK // 2), TOK // 2)]


def gelu_tanh(values):
    return jax.nn.gelu(values, approximate=True)


def rotary_tables():
    positions = jnp.arange(SEQ_LEN, dtype=jnp.float32)
    freqs = 10000.0 ** (-jnp.arange(ROT // 2, dtype=jnp.float32) * 2.0 / ROT)
    angles = positions[:, None] * freqs[None, :]
    return (jnp.cos(angles)[:, None, :], jnp.sin(angles)[:, None, :])


def rotate(values, cos_table, sin_table):
    half_rot = ROT // 2
    first_half = values[..., :half_rot]
    second = values[..., half_rot:ROT]
    return jnp.concatenate(
        [
            first_half * cos_table - second * sin_table,
            second * cos_table + first_half * sin_table,
            values[..., ROT:],
        ],
        axis=-1,
    )


def block_layout(seq_length):
    block_rows = min(512, seq_length)
    return (block_rows, seq_length // block_rows)


def masked_scores(q_block, rotated_keys, first_row, score_scale):
    block_rows = q_block.shape[0]
    key_pos = jnp.arange(rotated_keys.shape[0], dtype=jnp.int32)
    row_pos = first_row + jnp.arange(block_rows, dtype=jnp.int32)
    scores = (
        jnp.einsum("qhd,khd->hqk", q_block, rotated_keys, preferred_element_type=jnp.float32)
        * score_scale
    )
    return jnp.where((key_pos[None, :] <= row_pos[:, None])[None], scores, -1e30)


def attend_forward(queries, rotated_keys, values, score_scale):
    seq_length, head_count = (queries.shape[0], queries.shape[1])
    block_rows, block_count = block_layout(seq_length)
    q_blocks = queries.reshape(block_count, block_rows, head_count, HD)
    first_rows = jnp.arange(block_count, dtype=jnp.int32) * block_rows

    def one_block(block_item):
        q_block, first_row = block_item
        scores = masked_scores(q_block, rotated_keys, first_row, score_scale)
        row_max = jnp.max(scores, axis=-1, keepdims=True)
        exponents = jnp.exp(scores - row_max)
        row_sum = jnp.sum(exponents, axis=-1, keepdims=True)
        probs_low = (exponents / row_sum).astype(jnp.bfloat16)
        context = jnp.einsum("hqk,khd->qhd", probs_low, values, preferred_element_type=jnp.float32)
        return (context, (row_max + jnp.log(row_sum))[..., 0])

    contexts, logsums = lax.map(one_block, (q_blocks, first_rows))
    return (contexts.reshape(seq_length, head_count * HD), logsums)


def attend_backward(queries, rotated_keys, values, grad_context, logsums, score_scale):
    seq_length, head_count = (queries.shape[0], queries.shape[1])
    block_rows, block_count = block_layout(seq_length)
    q_blocks = queries.reshape(block_count, block_rows, head_count, HD)
    g_blocks = grad_context.reshape(block_count, block_rows, head_count, HD)
    first_rows = jnp.arange(block_count, dtype=jnp.int32) * block_rows

    def one_block(carry, block_item):
        key_grad, value_grad = carry
        q_block, g_block, lse_block, first_row = block_item
        scores = masked_scores(q_block, rotated_keys, first_row, score_scale)
        probs = jnp.exp(scores - lse_block[..., None])
        prob_grad = jnp.einsum("qhd,khd->hqk", g_block, values, preferred_element_type=jnp.float32)
        row_dot = jnp.sum(probs * prob_grad, axis=-1, keepdims=True)
        score_grad = (probs * (prob_grad - row_dot)).astype(jnp.bfloat16)
        query_grad = (
            jnp.einsum("hqk,khd->qhd", score_grad, rotated_keys, preferred_element_type=jnp.float32)
            * score_scale
        )
        key_grad = (
            key_grad
            + jnp.einsum("hqk,qhd->khd", score_grad, q_block, preferred_element_type=jnp.float32)
            * score_scale
        )
        value_grad = value_grad + jnp.einsum(
            "hqk,qhd->khd", probs.astype(jnp.bfloat16), g_block, preferred_element_type=jnp.float32
        )
        return ((key_grad, value_grad), query_grad)

    zeros_kv = jnp.zeros((seq_length, head_count, HD), jnp.float32)
    (key_grad, value_grad), query_grads = lax.scan(
        one_block, (zeros_kv, zeros_kv), (q_blocks, g_blocks, logsums, first_rows)
    )
    return (query_grads.reshape(seq_length, head_count, HD), key_grad, value_grad)


def gather_kernel(x_ref, cot_ref, vec_ref, wa_ref, wb_ref, n_out, g_out, wa_out, wb_out, vecs,
                  ssem, rsem, vs, vr, lsem):
    f, t = lax.axis_index("fsdp"), lax.axis_index("tp")
    tp, fs = Group("tp"), Group("fsdp")
    own = [
        pltpu.make_async_copy(cot_ref, g_out.at[t], lsem.at[0]),
        pltpu.make_async_copy(wa_ref, wa_out.at[f], lsem.at[1]),
        pltpu.make_async_copy(wb_ref, wb_block(wb_out)(f), lsem.at[2]),
        pltpu.make_async_copy(vec_ref, wb_block(vecs)(f), lsem.at[3]),
    ]
    for copy in own:
        copy.start()
    greet(all_peers(f, t))
    vec_slot = wb_block(vecs)
    own[3].wait()
    for d in range(1, 16):
        to = (lax.rem(f + d, 16), t)
        remote(vec_slot(f), vec_slot(f), vs.at[d], vr.at[d], to).start()
    ga = Gather(fs, lambda i: wa_out.at[i], wa_half(wa_out), ssem.at[0], rsem.at[0], sibling=True)
    gb = Gather(fs, wb_block(wb_out), wb_half(wb_out), ssem.at[1], rsem.at[1], sibling=True)
    gn = Gather(tp, lambda i: n_out.at[i], token_half(n_out), ssem.at[2], rsem.at[2])
    gg = Gather(tp, lambda i: g_out.at[i], token_half(g_out), ssem.at[3], rsem.at[3])
    own[1].wait()
    ga.start()
    for d in range(1, 16):
        source = lax.rem(f + 16 - d, 16)
        remote(vec_slot(source), vec_slot(source), vs.at[d], vr.at[d], (source, t)).wait_recv()

    @pl.loop(0, TOK // 16)
    def _(i):
        rows = pl.ds(pl.multiple_of(i * 16, 16), 16)
        xf = x_ref[rows, :].astype(F32)
        mean = jnp.mean(xf, axis=-1, keepdims=True)
        centered = xf - mean
        variance = jnp.mean(centered * centered, axis=-1, keepdims=True)
        normed = centered * lax.rsqrt(variance + EPS) * vecs[0:1, :] + vecs[1:2, :]
        n_out[t, rows, :] = normed.astype(BF16)

    gn.start()
    ga.pair()
    own[2].wait()
    gb.start()
    gn.pair()
    ga.near()
    gn.near()
    ga.near_other()
    gb.pair()
    gn.near_other()
    own[0].wait()
    gg.start()
    ga.far()
    gb.near()
    gn.far()
    gg.pair()
    gb.near_other()
    gg.near()
    gb.far()
    gg.near_other()
    gg.far()
    for op in (ga, gb, gn, gg):
        op.finish()
    for d in range(1, 16):
        to = (lax.rem(f + d, 16), t)
        remote(vec_slot(f), vec_slot(f), vs.at[d], vr.at[d], to).wait_send()


def gather(x, cot, vec, wa, wb):
    return pl.pallas_call(
        gather_kernel,
        out_shape=(
            jax.ShapeDtypeStruct((8, TOK, D), BF16),
            jax.ShapeDtypeStruct((8, TOK, D), BF16),
            jax.ShapeDtypeStruct((16, TOK, WA), BF16),
            jax.ShapeDtypeStruct((WB, D), BF16),
            jax.ShapeDtypeStruct((8, D), F32),
        ),
        in_specs=[VMEM] * 5,
        out_specs=(VMEM,) * 5,
        scratch_shapes=[
            pltpu.SemaphoreType.DMA((4, 17)),
            pltpu.SemaphoreType.DMA((4, 17)),
            pltpu.SemaphoreType.DMA((16,)),
            pltpu.SemaphoreType.DMA((16,)),
            pltpu.SemaphoreType.DMA((4,)),
        ],
        compiler_params=pltpu.CompilerParams(collective_id=0, has_side_effects=True, vmem_limit_bytes=60 * 2**20),
        name="gather_all",
    )(x, cot, vec, wa, wb)


def scatter_kernel(x_ref, cot_ref, vecs, o_in, n_in, wa_in, wb_in, db_ref,
                   out_ref, ig_ref, vec_out, wa_out, wb_out, db_out,
                   o_buf, n_buf, wa_buf, wb_buf, sib_a, sib_b, far_a, near_a, pair_a, far_b, near_b, pair_b,
                   far_o, near_o, pair_o, far_n, near_n, pair_n, part, v1, v2, dbs,
                   ssem, rsem, v1s, v1r, v2s, v2r, ds_, dr, lsem):
    f, t = lax.axis_index("fsdp"), lax.axis_index("tp")
    tp, fs = Group("tp"), Group("fsdp")
    local = [
        pltpu.make_async_copy(o_in, o_buf, lsem.at[0]),
        pltpu.make_async_copy(wb_in, wb_buf, lsem.at[1]),
        pltpu.make_async_copy(wa_in, wa_buf, lsem.at[2]),
        pltpu.make_async_copy(n_in, n_buf, lsem.at[3]),
    ]
    for copy in local:
        copy.start()
    dbs[f] = db_ref[...]
    greet(all_peers(f, t))
    for d in range(1, 16):
        remote(dbs.at[f], dbs.at[f], ds_.at[d], dr.at[d], (lax.rem(f + d, 16), t)).start()
    so = Scatter(tp, lambda i: o_buf.at[i], token_half(o_buf), far_o, near_o, pair_o, ssem.at[0], rsem.at[0], 16)
    sn = Scatter(tp, lambda i: n_buf.at[i], token_half(n_buf), far_n, near_n, pair_n, ssem.at[1], rsem.at[1], 16)
    sa = Scatter(fs, lambda i: wa_buf.at[i], wa_half(wa_buf), far_a, near_a, pair_a, ssem.at[2], rsem.at[2], 16, sib_a)
    sb = Scatter(fs, wb_block(wb_buf), wb_half(wb_buf), far_b, near_b, pair_b, ssem.at[3], rsem.at[3], 128, sib_b)
    local[0].wait()
    so.start()
    local[1].wait()
    sb.sib_start()
    local[2].wait()
    sa.sib_start()
    local[3].wait()
    sb.sib_add()
    sb.start()
    so.near(0)
    so.near(1)
    sn.start()
    sa.sib_add()
    sb.near(0)
    sa.start()
    sb.near(1)
    so.pair()
    sn.near(0)
    sb.pair()
    sa.near(0)
    sn.near(1)
    sa.near(1)
    refs = so.last()

    @pl.loop(0, TOK // 16)
    def _(i):
        rows = pl.ds(pl.multiple_of(i * 16, 16), 16)
        total = x_ref[rows, :].astype(F32) + vecs[2:3, :]
        for ref in refs:
            total = total + ref[rows, :].astype(F32)
        out_ref[rows, :] = total.astype(BF16)

    sn.pair()
    sa.pair()
    wb_refs = sb.last()
    add_rows(wb_out, wb_refs, 128)
    refs_n = sn.last()
    part[...] = jnp.zeros_like(part)

    @pl.loop(0, TOK // 16)
    def _(i):
        rows = pl.ds(pl.multiple_of(i * 16, 16), 16)
        xf = x_ref[rows, :].astype(F32)
        mean = jnp.mean(xf, axis=-1, keepdims=True)
        centered = xf - mean
        inv = lax.rsqrt(jnp.mean(centered * centered, axis=-1, keepdims=True) + EPS)
        xhat = centered * inv
        total = refs_n[0][rows, :].astype(F32)
        for ref in refs_n[1:]:
            total = total + ref[rows, :].astype(F32)
        e = total * vecs[0:1, :]
        back = (e - jnp.mean(e, axis=-1, keepdims=True) - xhat * jnp.mean(e * xhat, axis=-1, keepdims=True)) * inv
        cot = cot_ref[rows, :].astype(F32)
        ig_ref[rows, :] = (cot + back).astype(BF16)
        part[0:1, :] += jnp.sum(total * xhat, axis=0, keepdims=True)
        part[1:2, :] += jnp.sum(total, axis=0, keepdims=True)
        part[2:3, :] += jnp.sum(cot, axis=0, keepdims=True)

    piece = wb_block(part)
    for d in range(1, 16):
        to = lax.rem(f + d, 16)
        remote(piece(to), v1.at[f], v1s.at[d], v1r.at[d], (to, t)).start()
    v1[f] = part[:, pl.ds(pl.multiple_of(f * 128, 128), 128)]
    add_rows(wa_out, sa.last(), 16)
    for d in range(1, 16):
        source = lax.rem(f + 16 - d, 16)
        remote(dbs.at[source], dbs.at[source], ds_.at[d], dr.at[d], (source, t)).wait_recv()
    db_out[...] = jnp.sum(dbs[...], axis=0)
    for d in range(1, 16):
        source = lax.rem(f + 16 - d, 16)
        remote(piece(source), v1.at[source], v1s.at[d], v1r.at[d], (source, t)).wait_recv()
    v2[t] = jnp.sum(v1[...], axis=0)
    for d in range(1, 8):
        remote(v2.at[t], v2.at[t], v2s.at[d], v2r.at[d], (f, lax.rem(t + d, 8))).start()
    for d in range(1, 8):
        source = lax.rem(t + 8 - d, 8)
        remote(v2.at[source], v2.at[source], v2s.at[d], v2r.at[d], (f, source)).wait_recv()
    vec_out[...] = jnp.sum(v2[...], axis=0)
    for op in (so, sn, sa, sb):
        op.finish()
    for d in range(1, 16):
        to = lax.rem(f + d, 16)
        remote(dbs.at[f], dbs.at[f], ds_.at[d], dr.at[d], (to, t)).wait_send()
        remote(piece(to), v1.at[f], v1s.at[d], v1r.at[d], (to, t)).wait_send()
    for d in range(1, 8):
        remote(v2.at[t], v2.at[t], v2s.at[d], v2r.at[d], (f, lax.rem(t + d, 8))).wait_send()


def scatter(x, cot, vecs, o, n, wa, wb, db):
    def bufs(full, half):
        return [pltpu.VMEM((2, 2) + half, BF16), pltpu.VMEM((2, 2) + full, BF16), pltpu.VMEM(full, BF16)]

    dma = pltpu.SemaphoreType.DMA
    return pl.pallas_call(
        scatter_kernel,
        out_shape=(
            jax.ShapeDtypeStruct((TOK, D), BF16),
            jax.ShapeDtypeStruct((TOK, D), BF16),
            jax.ShapeDtypeStruct((8, 128), F32),
            jax.ShapeDtypeStruct((TOK, WA), F32),
            jax.ShapeDtypeStruct((WB, 128), F32),
            jax.ShapeDtypeStruct((16, 128), F32),
        ),
        in_specs=[VMEM, VMEM, VMEM, ANY, ANY, ANY, ANY, VMEM],
        out_specs=(VMEM,) * 6,
        scratch_shapes=[
            pltpu.VMEM((8, TOK, D), BF16),
            pltpu.VMEM((8, TOK, D), BF16),
            pltpu.VMEM((16, TOK, WA), BF16),
            pltpu.VMEM((WB, D), BF16),
            pltpu.VMEM((8, TOK, WA), BF16),
            pltpu.VMEM((8, WB, 128), BF16),
            *bufs((TOK, WA), (TOK // 2, WA)),
            *bufs((WB, 128), (WB // 2, 128)),
            *bufs((TOK, D), (TOK // 2, D)),
            *bufs((TOK, D), (TOK // 2, D)),
            pltpu.VMEM((8, D), F32),
            pltpu.VMEM((16, 8, 128), F32),
            pltpu.VMEM((8, 8, 128), F32),
            pltpu.VMEM((16, 16, 128), F32),
            dma((4, 17)), dma((4, 17)), dma((16,)), dma((16,)), dma((8,)), dma((8,)), dma((16,)), dma((16,)), dma((4,)),
        ],
        compiler_params=pltpu.CompilerParams(collective_id=1, has_side_effects=True, vmem_limit_bytes=60 * 2**20),
        name="scatter_all",
    )(x, cot, vecs, o, n, wa, wb, db)


def on_device(
    block_input, norm_gain, norm_bias, qkv_weight, qkv_bias, dense_weight, dense_bias, up_weight, up_bias,
    down_weight, down_bias, cotangent,
):
    zero = jnp.zeros((TOK,), F32)
    out_bias = dense_bias.astype(F32) + down_bias.astype(F32)
    vec = jnp.stack([norm_gain.astype(F32), norm_bias.astype(F32), out_bias, zero, zero, zero, zero, zero])
    wa = jnp.concatenate([qkv_weight.reshape(TOK, 768), up_weight], axis=1)
    wb = jnp.concatenate([dense_weight, down_weight], axis=0)
    n8, g8, wa16, wb_full, vecs = gather(block_input, cotangent, vec, wa, wb)
    normed = n8.reshape(SEQ_LEN, D)
    out_grad = g8.reshape(SEQ_LEN, D)
    wa_full = wa16.reshape(D, WA)
    bias_a = jnp.concatenate([qkv_bias.reshape(768), up_bias]).astype(F32)
    joined = jnp.dot(normed, wa_full, preferred_element_type=F32) + bias_a
    qkv, hidden = joined[:, :768].reshape(SEQ_LEN, 3, 4, HD), joined[:, 768:]
    cos_table, sin_table = rotary_tables()
    queries = rotate(qkv[:, 0], cos_table, sin_table).astype(BF16)
    keys = rotate(qkv[:, 1], cos_table, sin_table).astype(BF16)
    values = qkv[:, 2].astype(BF16)
    scale = HD**-0.5
    context, logsums = attend_forward(queries, keys, values, scale)
    active, gelu_pull = jax.vjp(gelu_tanh, hidden)
    a = jnp.concatenate([context.astype(BF16), active.astype(BF16)], axis=1)
    o = jnp.dot(a, wb_full, preferred_element_type=F32).astype(BF16)
    da = lax.dot_general(out_grad, wb_full, (((1,), (1,)), ((), ())), preferred_element_type=F32)
    dwb = lax.dot_general(a, out_grad, (((0,), (0,)), ((), ())), preferred_element_type=F32).astype(BF16)
    dhid = gelu_pull(da[:, 256:])[0].astype(BF16)
    dctx = da[:, :256].astype(BF16).reshape(SEQ_LEN, 4, HD)
    dq, dk, dv = attend_backward(queries, keys, values, dctx, logsums, scale)
    dq = rotate(dq, cos_table, -sin_table)
    dk = rotate(dk, cos_table, -sin_table)
    dqkv = jnp.stack([dq, dk, dv], axis=1).reshape(SEQ_LEN, 768).astype(BF16)
    dh = jnp.concatenate([dqkv, dhid], axis=1)
    dwa = lax.dot_general(normed, dh, (((0,), (0,)), ((), ())), preferred_element_type=F32).astype(BF16)
    dn = lax.dot_general(dh, wa_full, (((1,), (1,)), ((), ())), preferred_element_type=F32).astype(BF16)
    db = jnp.sum(dh.astype(F32), axis=0).reshape(14, 128)
    db = jnp.concatenate([db, jnp.zeros((2, 128), F32)], axis=0)
    block_output, input_grad, vec_grad, da_sum, db_sum, bias_sum = scatter(
        block_input, cotangent, vecs, o.reshape(8, TOK, D), dn.reshape(8, TOK, D),
        dwa.reshape(16, TOK, WA), dwb, db,
    )
    bias_sum = bias_sum.reshape(2048)
    return (
        block_output,
        input_grad,
        vec_grad[0],
        vec_grad[1],
        da_sum[:, :768].reshape(TOK, 3, 256),
        bias_sum[:768].reshape(3, 256),
        db_sum[:256],
        vec_grad[2],
        da_sum[:, 768:],
        bias_sum[768:1792],
        db_sum[256:],
        vec_grad[2],
    )


def solution(mesh):
    in_specs = (
        P(("fsdp", "tp"), None),
        P("fsdp"),
        P("fsdp"),
        P("fsdp", None, "tp"),
        P(None, "tp"),
        P("tp", "fsdp"),
        P("fsdp"),
        P("fsdp", "tp"),
        P("tp"),
        P("tp", "fsdp"),
        P("fsdp"),
        P(("fsdp", "tp"), None),
    )
    out_specs = (
        P(("fsdp", "tp"), None),
        P(("fsdp", "tp"), None),
        P("fsdp"),
        P("fsdp"),
        P("fsdp", None, "tp"),
        P(None, "tp"),
        P("tp", "fsdp"),
        P("fsdp"),
        P("fsdp", "tp"),
        P("tp"),
        P("tp", "fsdp"),
        P("fsdp"),
    )
    return jax.shard_map(
        on_device, mesh=mesh, in_specs=in_specs, out_specs=out_specs, check_vma=False
    )
```

```python
import jax
import jax.numpy as jnp
import numpy as np
from jax import lax
from jax.experimental import pallas as pl
from jax.experimental.pallas import tpu as pltpu
from jax.sharding import PartitionSpec as P

HD = 64
ROT = 32
SEQ_LEN = 1024
EPS = 1e-05
D = 2048
TOK = 128
WA = 1792
WB = 1280
GELU = 0.7978845608028654
F32 = jnp.float32
BF16 = jnp.bfloat16
MESH = pl.DeviceIdType.MESH
ANY = pl.BlockSpec(memory_space=pl.ANY)
VMEM = pl.BlockSpec(memory_space=pltpu.VMEM)


def place():
    f = lax.axis_index("fsdp")
    t = lax.axis_index("tp")
    return f, t, lax.div(f, 4), lax.rem(lax.div(f, 2), 2), lax.rem(f, 2), lax.div(t, 4), lax.rem(t, 4)


def greet(peers):
    barrier = pltpu.get_barrier_semaphore()
    for peer in peers:
        pl.semaphore_signal(barrier, inc=1, device_id=peer, device_id_type=MESH)
    pl.semaphore_wait(barrier, len(peers))


def all_peers(f, t):
    peers = [(lax.rem(f + d, 16), t) for d in range(1, 16)]
    return peers + [(f, lax.rem(t + d, 8)) for d in range(1, 8)]


def remote(src, dst, ssem, rsem, to):
    return pltpu.make_async_remote_copy(
        src_ref=src, dst_ref=dst, send_sem=ssem, recv_sem=rsem, device_id=to, device_id_type=MESH
    )


class Group:
    def __init__(self, axis):
        f, t, z, yl, c, yh, x = place()
        self.axis = axis
        if axis == "tp":
            self.k, self.r, self.c = x, yh, 0
            self.dev = lambda r, k: (f, r * 4 + k)
        else:
            self.k, self.r, self.c = z, yl, c
            self.dev = lambda r, k: ((k * 2 + r) * 2 + c, t)
            self.sib = ((z * 2 + yl) * 2 + 1 - c, t)
        self.up, self.down, self.far = lax.rem(self.k + 1, 4), lax.rem(self.k + 3, 4), lax.rem(self.k + 2, 4)
        self.other = 1 - self.r

    def index(self, r, k, c=None):
        if self.axis == "tp":
            return r * 4 + k
        return (k * 2 + r) * 2 + (self.c if c is None else c)


class Gather:
    def __init__(self, group, block, half, ssem, rsem, sibling=False):
        g = self.g = group
        self.ssem, self.rsem = ssem, rsem
        self.sibling = sibling
        own = block(g.index(g.r, g.k))
        self.plan = {
            0: (own, block(g.index(g.other, g.k)), g.dev(g.other, g.k)),
            1: (own, block(g.index(g.r, g.down)), g.dev(g.r, g.up)),
            2: (own, block(g.index(g.r, g.up)), g.dev(g.r, g.down)),
            3: (block(g.index(g.other, g.k)), block(g.index(g.other, g.down)), g.dev(g.r, g.up)),
            4: (block(g.index(g.other, g.k)), block(g.index(g.other, g.up)), g.dev(g.r, g.down)),
            5: (half(g.index(g.r, g.down), 0), half(g.index(g.r, g.far), 0), g.dev(g.r, g.up)),
            6: (half(g.index(g.r, g.up), 1), half(g.index(g.r, g.far), 1), g.dev(g.r, g.down)),
            7: (half(g.index(g.other, g.down), 0), half(g.index(g.other, g.far), 0), g.dev(g.r, g.up)),
            8: (half(g.index(g.other, g.up), 1), half(g.index(g.other, g.far), 1), g.dev(g.r, g.down)),
        }
        if sibling:
            order = [(g.r, g.k), (g.other, g.k), (g.r, g.down), (g.r, g.up)]
            order += [(g.other, g.down), (g.other, g.up), (g.r, g.far), (g.other, g.far)]
            for n, (r, k) in enumerate(order):
                self.plan[9 + n] = (block(g.index(r, k)), block(g.index(r, k, 1 - g.c)), g.sib)

    def send(self, n):
        src, _, to = self.plan[n]
        remote(src, src, self.ssem.at[n], self.rsem.at[n], to).start()

    def recv(self, n):
        src, dst, to = self.plan[n]
        remote(dst, dst, self.ssem.at[n], self.rsem.at[n], to).wait_recv()

    def pass_on(self, n):
        if self.sibling:
            self.send(n)

    def start(self):
        for n in (0, 1, 2):
            self.send(n)
        self.pass_on(9)

    def pair(self):
        self.recv(0)
        self.send(3)
        self.send(4)
        self.pass_on(10)

    def near(self):
        self.recv(1)
        self.send(5)
        self.recv(2)
        self.send(6)
        self.pass_on(11)
        self.pass_on(12)

    def near_other(self):
        self.recv(3)
        self.send(7)
        self.recv(4)
        self.send(8)
        self.pass_on(13)
        self.pass_on(14)

    def far(self):
        self.recv(5)
        self.recv(6)
        self.pass_on(15)
        self.recv(7)
        self.recv(8)
        self.pass_on(16)

    def finish(self):
        if self.sibling:
            for n in range(9, 17):
                self.recv(n)
        for n, (src, _, to) in self.plan.items():
            remote(src, src, self.ssem.at[n], self.rsem.at[n], to).wait_send()


def add_rows(out, ins, chunk):
    @pl.loop(0, out.shape[0] // chunk)
    def _(i):
        rows = pl.ds(pl.multiple_of(i * chunk, chunk), chunk)
        total = ins[0][rows, :].astype(F32)
        for ref in ins[1:]:
            total = total + ref[rows, :].astype(F32)
        out[rows, :] = total.astype(out.dtype)


def dot_nn(a, b):
    return jnp.dot(a, b, preferred_element_type=F32)


def dot_nt(a, b):
    return lax.dot_general(a, b, (((1,), (1,)), ((), ())), preferred_element_type=F32)


def dot_tn(a, b):
    return lax.dot_general(a, b, (((0,), (0,)), ((), ())), preferred_element_type=F32)


def rotary_rows():
    lane = np.arange(128) % HD
    freqs = (10000.0 ** (-np.arange(ROT // 2) * 2.0 / ROT)).astype(np.float32)
    angle = np.arange(SEQ_LEN, dtype=np.float32)[:, None] * freqs[lane % (ROT // 2)][None, :]
    turned = lane < ROT
    cos = np.where(turned, np.cos(angle), 1.0)
    sin = np.where(turned, np.sin(angle) * np.where(lane < ROT // 2, -1.0, 1.0), 0.0)
    return np.stack([cos, sin]).astype(np.float32)


def turn(values, cos, sin):
    lane = lax.broadcasted_iota(jnp.int32, values.shape, 1)
    first = lax.rem(lane, HD) < ROT // 2
    partner = jnp.where(first, pltpu.roll(values, 240, 1), pltpu.roll(values, 16, 1))
    return values * cos + partner * sin


def tables(tab, rows):
    cos, sin = tab[0, rows, :], tab[1, rows, :]
    return jnp.concatenate([cos, cos], axis=1), jnp.concatenate([sin, sin], axis=1)


def head_lanes(h, rows):
    lane = lax.broadcasted_iota(jnp.int32, (rows, 256), 1)
    return lax.div(lane, HD) == h


RB = 256


def rows_of(i):
    return pl.ds(pl.multiple_of(i * RB, RB), RB)


def project(i, n, wa, bias, tab, q, k, v, a, dh):
    rows = rows_of(i)
    cos, sin = tables(tab, rows)
    joined = dot_nn(n[rows, :], wa[...]) + bias[0:1, :]
    q[rows, :] = (turn(joined[:, :256], cos, sin) * HD**-0.5).astype(BF16)
    k[rows, :] = turn(joined[:, 256:512], cos, sin).astype(BF16)
    v[rows, :] = joined[:, 512:768].astype(BF16)
    z = joined[:, 768:]
    z2 = z * z
    th = jnp.tanh(z * (GELU + (GELU * 0.044715) * z2))
    half = 0.5 + 0.5 * th
    a[rows, 256:] = (z * half).astype(BF16)
    dh[rows, 768:] = (half + (half - half * half) * z * (2 * GELU + (6 * GELU * 0.044715) * z2)).astype(BF16)


def attend(i, q, k, v, a, lse):
    rows, before = slice(i * RB, (i + 1) * RB), i * RB
    qb = q[rows, :]
    causal = lax.broadcasted_iota(jnp.int32, (RB, RB), 1) <= lax.broadcasted_iota(jnp.int32, (RB, RB), 0)
    lane = lax.broadcasted_iota(jnp.int32, (RB, 128), 1)
    context = jnp.zeros((RB, 256), F32)
    logs = jnp.zeros((RB, 128), F32)
    for h in range(4):
        mine = head_lanes(h, RB)
        qh = jnp.where(mine, qb, jnp.zeros_like(qb))
        s1 = jnp.where(causal, dot_nt(qh, k[rows, :]), -1e30)
        top = jnp.max(s1, axis=1, keepdims=True)
        if i:
            s0 = dot_nt(qh, k[:before, :])
            top = jnp.maximum(top, jnp.max(s0, axis=1, keepdims=True))
        p1 = jnp.exp(s1 - top)
        total = jnp.sum(p1, axis=1, keepdims=True)
        out = dot_nn(p1.astype(BF16), v[rows, :])
        if i:
            p0 = jnp.exp(s0 - top)
            total = total + jnp.sum(p0, axis=1, keepdims=True)
            out = out + dot_nn(p0.astype(BF16), v[:before, :])
        context = jnp.where(mine, out / total, context)
        logs = jnp.where(lane == h, top + jnp.log(total), logs)
    a[rows, :256] = context.astype(BF16)
    lse[rows, :] = logs


def attend_back(i, q, k, v, lse, tab, dh, dk, dv, ps, ds, gs):
    rows, width = slice(i * RB, (i + 1) * RB), (i + 1) * RB
    qb, gb = q[rows, :], dh[rows, :256]
    causal = lax.broadcasted_iota(jnp.int32, (RB, RB), 1) <= lax.broadcasted_iota(jnp.int32, (RB, RB), 0)
    dq = jnp.zeros((RB, 256), F32)
    for h in range(4):
        mine = head_lanes(h, RB)
        part = slice(h * RB, (h + 1) * RB)
        qh = jnp.where(mine, qb, jnp.zeros_like(qb))
        gh = jnp.where(mine, gb, jnp.zeros_like(gb))
        ps[part, SEQ_LEN:] = qh
        gs[part, :] = gh
        log = lse[rows, h : h + 1]
        s = dot_nt(qh, k[:width, :])
        if i:
            s = jnp.concatenate([s[:, : i * RB], jnp.where(causal, s[:, i * RB :], -1e30)], axis=1)
        else:
            s = jnp.where(causal, s, -1e30)
        p = jnp.exp(s - log)
        t = p * dot_nt(gh, v[:width, :])
        row = jnp.sum(t, axis=1, keepdims=True)
        low = (t - p * row).astype(BF16)
        ps[part, :width] = p.astype(BF16)
        ds[part, :width] = low
        dq = jnp.where(mine, dot_nn(low, k[:width, :]), dq)
    key = dot_tn(ds[:, :width], ps[:, SEQ_LEN:])
    val = dot_tn(ps[:, :width], gs[...])
    if i == 3:
        dk[...] = key
        dv[...] = val
    else:
        dk[:width, :] += key
        dv[:width, :] += val
    cos, sin = tables(tab, rows)
    dh[rows, :256] = turn(dq * HD**-0.5, cos, -sin).astype(BF16)


def keys_back(tab, dh, dk, dv):
    @pl.loop(0, 4)
    def _(i):
        rows = rows_of(i)
        cos, sin = tables(tab, rows)
        dh[rows, 256:512] = turn(dk[rows, :], cos, -sin).astype(BF16)
        dh[rows, 512:768] = dv[rows, :].astype(BF16)


def branch_out(i, a, wb, o):
    rows = rows_of(i)
    o[rows, :] = dot_nn(a[rows, :], wb[...]).astype(BF16)


def branch_back(i, g, wb, dh):
    rows = rows_of(i)
    back = dot_nt(g[rows, :], wb[...])
    dh[rows, :256] = back[:, :256].astype(BF16)
    dh[rows, 768:] = (back[:, 256:] * dh[rows, 768:].astype(F32)).astype(BF16)


def columns_of(m):
    return pl.ds(pl.multiple_of(m * 256, 256), 256)


def grad_wb(m, a, g, wb):
    cols = columns_of(m)
    wb[:, cols] = dot_tn(a[...], g[:, cols]).astype(BF16)


def normed_back(i, dh, wa, out):
    rows = rows_of(i)
    out[rows, :] = dot_nt(dh[rows, :], wa[...]).astype(BF16)


def grad_wa(m, n, dh, wa):
    cols = columns_of(m)
    wa[cols, :] = dot_tn(n[:, cols], dh[...]).astype(BF16)


def grad_bias(dh, put):
    total = jnp.sum(dh[0:RB, :].astype(F32), axis=0, keepdims=True)
    for i in range(1, 4):
        total = total + jnp.sum(dh[i * RB : (i + 1) * RB, :].astype(F32), axis=0, keepdims=True)
    for j in range(WA // 128):
        put(j, total[:, j * 128 : (j + 1) * 128])


class Scatter:
    def __init__(self, group, block, half, far, near, pair, ssem, rsem, chunk, sib=None):
        g = self.g = group
        self.block, self.half, self.chunk = block, half, chunk
        self.far_ref, self.near_ref, self.pair_ref, self.sib_ref = far, near, pair, sib
        self.ssem, self.rsem = ssem, rsem
        self.order = [(g.other, g.far), (g.r, g.far), (g.other, g.up), (g.other, g.down)]
        self.order += [(g.r, g.up), (g.r, g.down), (g.other, g.k), (g.r, g.k)]
        self.plan = {}
        for n, r in ((0, g.other), (4, g.r)):
            slot = n // 4
            self.plan[n] = (half(g.index(r, g.far), 0), far.at[slot, 0], g.dev(g.r, g.up))
            self.plan[n + 1] = (half(g.index(r, g.far), 1), far.at[slot, 1], g.dev(g.r, g.down))
            self.plan[n + 2] = (block(g.index(r, g.up)), near.at[slot, 0], g.dev(g.r, g.up))
            self.plan[n + 3] = (block(g.index(r, g.down)), near.at[slot, 1], g.dev(g.r, g.down))
        self.plan[8] = (block(g.index(g.other, g.k)), pair, g.dev(g.other, g.k))
        if sib is not None:
            for s, (r, k) in enumerate(self.order):
                self.plan[9 + s] = (block(g.index(r, k, 1 - g.c)), sib.at[s], g.sib)

    def chip(self, s):
        r, k = self.order[s]
        return k * 2 + r

    def send(self, n):
        src, dst, to = self.plan[n]
        remote(src, dst, self.ssem.at[n], self.rsem.at[n], to).start()

    def recv(self, n):
        src, dst, to = self.plan[n]
        remote(src, dst, self.ssem.at[n], self.rsem.at[n], to).wait_recv()

    def sib_send(self, s):
        self.send(9 + s)

    def sib_add(self, s):
        self.recv(9 + s)
        mine = self.block(self.g.index(*self.order[s]))
        add_rows(mine, [mine, self.sib_ref.at[s]], self.chunk)

    def step(self, s):
        if s < 2:
            self.send(4 * s)
            self.send(4 * s + 1)
        elif s < 6:
            slot, way = (s - 2) // 2, s % 2
            n = 4 * slot + way
            self.recv(n)
            mine = self.half(self.g.index(*self.order[s]), way)
            add_rows(mine, [mine, self.far_ref.at[slot, way]], self.chunk)
            self.send(n + 2)
        else:
            self.recv(2)
            self.recv(3)
            mine = self.block(self.g.index(*self.order[6]))
            add_rows(mine, [mine, self.near_ref.at[0, 0], self.near_ref.at[0, 1]], self.chunk)
            self.send(8)

    def steps(self, *numbers):
        for s in numbers:
            self.step(s)

    def last(self):
        for n in (6, 7, 8):
            self.recv(n)
        return [self.block(self.g.index(*self.order[7])), self.near_ref.at[1, 0], self.near_ref.at[1, 1], self.pair_ref]

    def finish(self):
        for n, (src, dst, to) in self.plan.items():
            remote(src, dst, self.ssem.at[n], self.rsem.at[n], to).wait_send()


def row_block(ref):
    return lambda i: ref.at[pl.ds(pl.multiple_of(i * TOK, TOK), TOK)]


def row_half(ref):
    return lambda i, h: ref.at[pl.ds(pl.multiple_of(i * TOK + h * (TOK // 2), TOK // 2), TOK // 2)]


def col_block(ref):
    return lambda i: ref.at[:, pl.ds(pl.multiple_of(i * 128, 128), 128)]


def col_half(ref):
    return lambda i, h: ref.at[pl.ds(h * (WB // 2), WB // 2), pl.ds(pl.multiple_of(i * 128, 128), 128)]


def sixteen_rows(i):
    return pl.ds(pl.multiple_of(i * 16, 16), 16)


def load_rows(src, dst, sem):
    copies = [pltpu.make_async_copy(src.at[pl.ds(j * 64, 64)], dst.at[j], sem.at[j]) for j in range(2)]
    for copy in copies:
        copy.start()
    return copies


def loaded(ref, i):
    return ref[lax.div(i, 4), pl.ds(pl.multiple_of(lax.rem(i, 4) * 16, 16), 16), :].astype(F32)


def block_kernel(x_ref, cot_ref, vec_ref, qkv_ref, up_ref, dense_ref, down_ref, bias, tab_ref,
                 out_ref, ig_ref, vec_out, dqkv_out, dup_out, ddense_out, ddown_out, db_out,
                 n, g, wa, wb, vecs, o, q, k, v, a, dh, lse, dk, dv, ds, gs, tab,
                 sib_a, sib_b, far_a, near_a, pair_a, far_b, near_b, pair_b, far_o, near_o, pair_o, far_n, near_n, pair_n,
                 part, v1, v2, dbs, ssem, rsem, v0s, v0r, v1s, v1r, v2s, v2r, dss, dsr, lsem):
    f, t = lax.axis_index("fsdp"), lax.axis_index("tp")
    tp, fs = Group("tp"), Group("fsdp")
    wa_own, wb_own = row_block(wa)(f), col_block(wb)(f)
    vec_slot = col_block(vecs)
    own = [
        pltpu.make_async_copy(vec_ref, vec_slot(f), lsem.at[0]),
        pltpu.make_async_copy(qkv_ref, wa_own.at[:, pl.ds(0, 768)], lsem.at[1]),
        pltpu.make_async_copy(up_ref, wa_own.at[:, pl.ds(768, 1024)], lsem.at[2]),
        pltpu.make_async_copy(dense_ref, wb_own.at[pl.ds(0, 256)], lsem.at[3]),
        pltpu.make_async_copy(down_ref, wb_own.at[pl.ds(256, 1024)], lsem.at[4]),
        pltpu.make_async_copy(cot_ref, row_block(g)(t), lsem.at[5]),
        pltpu.make_async_copy(tab_ref, tab, lsem.at[6]),
    ]
    for copy in own:
        copy.start()
    rows_in = load_rows(x_ref, far_n.at[0], lsem.at[pl.ds(20, 2)])
    greet(all_peers(f, t))
    own[0].wait()
    for d in range(1, 16):
        remote(vec_slot(f), vec_slot(f), v0s.at[d], v0r.at[d], (lax.rem(f + d, 16), t)).start()
    ga = Gather(fs, row_block(wa), row_half(wa), ssem.at[0], rsem.at[0], sibling=True)
    gb = Gather(fs, col_block(wb), col_half(wb), ssem.at[1], rsem.at[1], sibling=True)
    gn = Gather(tp, row_block(n), row_half(n), ssem.at[2], rsem.at[2])
    gg = Gather(tp, row_block(g), row_half(g), ssem.at[3], rsem.at[3])
    so = Scatter(tp, row_block(o), row_half(o), far_o, near_o, pair_o, ssem.at[4], rsem.at[4], 16)
    sn = Scatter(tp, row_block(g), row_half(g), far_n, near_n, pair_n, ssem.at[5], rsem.at[5], 16)
    sa = Scatter(fs, row_block(wa), row_half(wa), far_a, near_a, pair_a, ssem.at[6], rsem.at[6], 16, sib_a)
    sb = Scatter(fs, col_block(wb), col_half(wb), far_b, near_b, pair_b, ssem.at[7], rsem.at[7], 128, sib_b)
    own[1].wait()
    own[2].wait()
    ga.start()
    for d in range(1, 16):
        source = lax.rem(f + 16 - d, 16)
        remote(vec_slot(source), vec_slot(source), v0s.at[d], v0r.at[d], (source, t)).wait_recv()

    for copy in rows_in:
        copy.wait()

    @pl.loop(0, TOK // 16)
    def _(i):
        xf = loaded(far_n.at[0], i)
        mean = jnp.mean(xf, axis=-1, keepdims=True)
        centered = xf - mean
        variance = jnp.mean(centered * centered, axis=-1, keepdims=True)
        normed = centered * lax.rsqrt(variance + EPS) * vecs[0:1, :] + vecs[1:2, :]
        n[pl.ds(pl.multiple_of(t * TOK + i * 16, 16), 16), :] = normed.astype(BF16)

    gn.start()
    ga.pair()
    own[3].wait()
    own[4].wait()
    gn.pair()
    ga.near()
    gb.start()
    gn.near()
    ga.near_other()
    own[5].wait()
    gn.near_other()
    gg.start()
    gb.pair()
    ga.far()
    gn.far()
    ga.finish()
    own[6].wait()
    project(0, n, wa, bias, tab, q, k, v, a, dh)
    gb.near()
    project(1, n, wa, bias, tab, q, k, v, a, dh)
    gg.pair()
    project(2, n, wa, bias, tab, q, k, v, a, dh)
    gb.near_other()
    project(3, n, wa, bias, tab, q, k, v, a, dh)
    gg.near()
    attend(0, q, k, v, a, lse)
    attend(1, q, k, v, a, lse)
    gb.far()
    attend(2, q, k, v, a, lse)
    attend(3, q, k, v, a, lse)
    gb.finish()

    @pl.loop(0, 4)
    def _(i):
        branch_out(i, a, wb, o)

    gg.near_other()
    so.steps(0, 1)
    gg.far()
    gg.finish()

    @pl.loop(0, 4)
    def _(i):
        branch_back(i, g, wb, dh)

    so.steps(2, 3)
    for s in range(8):
        grad_wb(sb.chip(s), a, g, wb)
        sb.sib_send(s)
        if s > 0:
            sb.sib_add(s - 1)
        if s == 1:
            sb.step(0)
        if s == 2:
            sb.step(1)
        if s == 4:
            so.steps(4, 5)
    sb.sib_add(7)
    attend_back(3, q, k, v, lse, tab, dh, dk, dv, a, ds, gs)
    sb.steps(2, 3)
    attend_back(2, q, k, v, lse, tab, dh, dk, dv, a, ds, gs)
    sb.steps(4, 5)
    attend_back(1, q, k, v, lse, tab, dh, dk, dv, a, ds, gs)
    so.step(6)
    attend_back(0, q, k, v, lse, tab, dh, dk, dv, a, ds, gs)
    keys_back(tab, dh, dk, dv)

    @pl.loop(0, 4)
    def _(i):
        normed_back(i, dh, wa, g)

    sn.steps(0, 1)

    def put(j, row):
        dbs[f, j : j + 1, :] = row

    grad_bias(dh, put)
    dbs[f, WA // 128 :, :] = jnp.zeros((16 - WA // 128, 128), F32)
    for d in range(1, 16):
        remote(dbs.at[f], dbs.at[f], dss.at[d], dsr.at[d], (lax.rem(f + d, 16), t)).start()
    sb.step(6)
    for s in range(8):
        grad_wa(sa.chip(s), n, dh, wa)
        sa.sib_send(s)
        if s > 0:
            sa.sib_add(s - 1)
        if s == 1:
            sa.step(0)
        if s == 2:
            sa.step(1)
        if s == 4:
            sn.steps(2, 3)
        if s == 6:
            sn.steps(4, 5)
    sa.sib_add(7)
    out_refs = so.last()
    rows_in = load_rows(x_ref, far_o.at[1], lsem.at[pl.ds(20, 2)])
    for copy in rows_in:
        copy.wait()

    @pl.loop(0, TOK // 16)
    def _(i):
        rows = sixteen_rows(i)
        total = loaded(far_o.at[1], i) + vecs[2:3, :]
        for ref in out_refs:
            total = total + ref[rows, :].astype(F32)
        pair_o[rows, :] = total.astype(BF16)

    results = [pltpu.make_async_copy(pair_o, out_ref, lsem.at[7])]
    results[0].start()
    cots = load_rows(cot_ref, far_o.at[0], lsem.at[pl.ds(18, 2)])

    sa.steps(2, 3)
    sb_refs = sb.last()
    dense_sum, down_sum = dk.at[pl.ds(0, 256), pl.ds(128, 128)], dk.at[:, pl.ds(0, 128)]
    add_rows(dense_sum, [ref.at[pl.ds(0, 256)] for ref in sb_refs], 128)
    add_rows(down_sum, [ref.at[pl.ds(256, 1024)] for ref in sb_refs], 128)
    results.append(pltpu.make_async_copy(dense_sum, ddense_out, lsem.at[8]))
    results.append(pltpu.make_async_copy(down_sum, ddown_out, lsem.at[9]))
    results[1].start()
    results[2].start()
    sa.steps(4, 5)
    sn.step(6)
    sa.step(6)
    n_refs = sn.last()
    part[...] = jnp.zeros_like(part)
    for copy in cots:
        copy.wait()

    @pl.loop(0, TOK // 16)
    def _(i):
        rows = sixteen_rows(i)
        xf = loaded(far_o.at[1], i)
        centered = xf - jnp.mean(xf, axis=-1, keepdims=True)
        inv = lax.rsqrt(jnp.mean(centered * centered, axis=-1, keepdims=True) + EPS)
        xhat = centered * inv
        total = n_refs[0][rows, :].astype(F32)
        for ref in n_refs[1:]:
            total = total + ref[rows, :].astype(F32)
        e = total * vecs[0:1, :]
        back = (e - jnp.mean(e, axis=-1, keepdims=True) - xhat * jnp.mean(e * xhat, axis=-1, keepdims=True)) * inv
        cot = loaded(far_o.at[0], i)
        pair_n[rows, :] = (cot + back).astype(BF16)
        part[0:1, :] += jnp.sum(total * xhat, axis=0, keepdims=True)
        part[1:2, :] += jnp.sum(total, axis=0, keepdims=True)
        part[2:3, :] += jnp.sum(cot, axis=0, keepdims=True)

    results.append(pltpu.make_async_copy(pair_n, ig_ref, lsem.at[10]))
    results[3].start()
    piece = col_block(part)
    for d in range(1, 16):
        to = lax.rem(f + d, 16)
        remote(piece(to), v1.at[f], v1s.at[d], v1r.at[d], (to, t)).start()
    v1[f] = part[:, pl.ds(pl.multiple_of(f * 128, 128), 128)]
    for d in range(1, 16):
        source = lax.rem(f + 16 - d, 16)
        remote(dbs.at[source], dbs.at[source], dss.at[d], dsr.at[d], (source, t)).wait_recv()
    db_out[...] = jnp.sum(dbs[...], axis=0)
    for d in range(1, 16):
        source = lax.rem(f + 16 - d, 16)
        remote(piece(source), v1.at[source], v1s.at[d], v1r.at[d], (source, t)).wait_recv()
    v2[t] = jnp.sum(v1[...], axis=0)
    for d in range(1, 8):
        remote(v2.at[t], v2.at[t], v2s.at[d], v2r.at[d], (f, lax.rem(t + d, 8))).start()
    sa_refs = sa.last()
    for j in range(7):
        here = dv.at[pl.ds(j * TOK, TOK)]
        add_rows(here, [ref.at[:, pl.ds(j * 256, 256)] for ref in sa_refs], TOK)
        there = dqkv_out.at[:, pl.ds(j * 256, 256)] if j < 3 else dup_out.at[:, pl.ds((j - 3) * 256, 256)]
        results.append(pltpu.make_async_copy(here, there, lsem.at[11 + j]))
        results[-1].start()
    for d in range(1, 8):
        source = lax.rem(t + 8 - d, 8)
        remote(v2.at[source], v2.at[source], v2s.at[d], v2r.at[d], (f, source)).wait_recv()
    vec_out[...] = jnp.sum(v2[...], axis=0)
    for copy in results:
        copy.wait()
    for op in (gn, so, sn, sa, sb):
        op.finish()
    for d in range(1, 16):
        to = lax.rem(f + d, 16)
        remote(vec_slot(f), vec_slot(f), v0s.at[d], v0r.at[d], (to, t)).wait_send()
        remote(dbs.at[f], dbs.at[f], dss.at[d], dsr.at[d], (to, t)).wait_send()
        remote(piece(to), v1.at[f], v1s.at[d], v1r.at[d], (to, t)).wait_send()
    for d in range(1, 8):
        remote(v2.at[t], v2.at[t], v2s.at[d], v2r.at[d], (f, lax.rem(t + d, 8))).wait_send()


def run_block(x, cot, vec, qkv, up, dense, down, bias, tab):
    def bufs(full, half):
        return [pltpu.VMEM((2, 2) + half, BF16), pltpu.VMEM((2, 2) + full, BF16), pltpu.VMEM(full, BF16)]

    dma = pltpu.SemaphoreType.DMA
    sds = jax.ShapeDtypeStruct
    return pl.pallas_call(
        block_kernel,
        out_shape=(
            sds((TOK, D), BF16),
            sds((TOK, D), BF16),
            sds((8, 128), F32),
            sds((TOK, 768), F32),
            sds((TOK, 1024), F32),
            sds((256, 128), F32),
            sds((1024, 128), F32),
            sds((16, 128), F32),
        ),
        in_specs=[ANY, ANY, ANY, ANY, ANY, ANY, ANY, VMEM, ANY],
        out_specs=(ANY, ANY, VMEM, ANY, ANY, ANY, ANY, VMEM),
        scratch_shapes=[
            pltpu.VMEM((SEQ_LEN, D), BF16),
            pltpu.VMEM((SEQ_LEN, D), BF16),
            pltpu.VMEM((D, WA), BF16),
            pltpu.VMEM((WB, D), BF16),
            pltpu.VMEM((8, D), F32),
            pltpu.VMEM((SEQ_LEN, D), BF16),
            pltpu.VMEM((SEQ_LEN, 256), BF16),
            pltpu.VMEM((SEQ_LEN, 256), BF16),
            pltpu.VMEM((SEQ_LEN, 256), BF16),
            pltpu.VMEM((SEQ_LEN, WB), BF16),
            pltpu.VMEM((SEQ_LEN, WA), BF16),
            pltpu.VMEM((SEQ_LEN, 128), F32),
            pltpu.VMEM((SEQ_LEN, 256), F32),
            pltpu.VMEM((SEQ_LEN, 256), F32),
            pltpu.VMEM((SEQ_LEN, SEQ_LEN), BF16),
            pltpu.VMEM((SEQ_LEN, 256), BF16),
            pltpu.VMEM((2, SEQ_LEN, 128), F32),
            pltpu.VMEM((8, TOK, WA), BF16),
            pltpu.VMEM((8, WB, 128), BF16),
            *bufs((TOK, WA), (TOK // 2, WA)),
            *bufs((WB, 128), (WB // 2, 128)),
            *bufs((TOK, D), (TOK // 2, D)),
            *bufs((TOK, D), (TOK // 2, D)),
            pltpu.VMEM((8, D), F32),
            pltpu.VMEM((16, 8, 128), F32),
            pltpu.VMEM((8, 8, 128), F32),
            pltpu.VMEM((16, 16, 128), F32),
            dma((8, 17)), dma((8, 17)),
            dma((16,)), dma((16,)), dma((16,)), dma((16,)), dma((8,)), dma((8,)), dma((16,)), dma((16,)), dma((22,)),
        ],
        compiler_params=pltpu.CompilerParams(collective_id=0, has_side_effects=True, vmem_limit_bytes=64 * 2**20 - 2**18),
        name="block_all",
    )(x, cot, vec, qkv, up, dense, down, bias, tab)


def on_device(
    block_input, norm_gain, norm_bias, qkv_weight, qkv_bias, dense_weight, dense_bias, up_weight, up_bias,
    down_weight, down_bias, cotangent,
):
    zero = jnp.zeros((TOK,), F32)
    out_bias = dense_bias.astype(F32) + down_bias.astype(F32)
    vec = jnp.stack([norm_gain.astype(F32), norm_bias.astype(F32), out_bias, zero, zero, zero, zero, zero])
    bias = jnp.concatenate([qkv_bias.reshape(768), up_bias]).astype(F32).reshape(1, WA)
    block_output, input_grad, vec_grad, dqkv, dup, ddense, ddown, bias_sum = run_block(
        block_input, cotangent, vec, qkv_weight.reshape(TOK, 768), up_weight, dense_weight, down_weight, bias,
        jnp.asarray(rotary_rows()),
    )
    bias_sum = bias_sum.reshape(2048)
    return (
        block_output,
        input_grad,
        vec_grad[0],
        vec_grad[1],
        dqkv.reshape(TOK, 3, 256),
        bias_sum[:768].reshape(3, 256),
        ddense,
        vec_grad[2],
        dup,
        bias_sum[768:1792],
        ddown,
        vec_grad[2],
    )


def solution(mesh):
    in_specs = (
        P(("fsdp", "tp"), None),
        P("fsdp"),
        P("fsdp"),
        P("fsdp", None, "tp"),
        P(None, "tp"),
        P("tp", "fsdp"),
        P("fsdp"),
        P("fsdp", "tp"),
        P("tp"),
        P("tp", "fsdp"),
        P("fsdp"),
        P(("fsdp", "tp"), None),
    )
    out_specs = (
        P(("fsdp", "tp"), None),
        P(("fsdp", "tp"), None),
        P("fsdp"),
        P("fsdp"),
        P("fsdp", None, "tp"),
        P(None, "tp"),
        P("tp", "fsdp"),
        P("fsdp"),
        P("fsdp", "tp"),
        P("tp"),
        P("tp", "fsdp"),
        P("fsdp"),
    )
    return jax.shard_map(
        on_device, mesh=mesh, in_specs=in_specs, out_specs=out_specs, check_vma=False
    )
```

```python
import jax
import jax.numpy as jnp
import numpy as np
from jax import lax
from jax.experimental import pallas as pl
from jax.experimental.pallas import tpu as pltpu
from jax.sharding import PartitionSpec as P

HD = 64
ROT = 32
SEQ_LEN = 1024
EPS = 1e-05
D = 2048
TOK = 128
WA = 1792
WB = 1280
GELU = 0.7978845608028654
F32 = jnp.float32
BF16 = jnp.bfloat16
MESH = pl.DeviceIdType.MESH
ANY = pl.BlockSpec(memory_space=pl.ANY)
VMEM = pl.BlockSpec(memory_space=pltpu.VMEM)


def place():
    f = lax.axis_index("fsdp")
    t = lax.axis_index("tp")
    return f, t, lax.div(f, 4), lax.rem(lax.div(f, 2), 2), lax.rem(f, 2), lax.div(t, 4), lax.rem(t, 4)


def greet(peers):
    barrier = pltpu.get_barrier_semaphore()
    for peer in peers:
        pl.semaphore_signal(barrier, inc=1, device_id=peer, device_id_type=MESH)
    pl.semaphore_wait(barrier, len(peers))


def all_peers(f, t):
    peers = [(lax.rem(f + d, 16), t) for d in range(1, 16)]
    return peers + [(f, lax.rem(t + d, 8)) for d in range(1, 8)]


def remote(src, dst, ssem, rsem, to):
    return pltpu.make_async_remote_copy(
        src_ref=src, dst_ref=dst, send_sem=ssem, recv_sem=rsem, device_id=to, device_id_type=MESH
    )


class Group:
    def __init__(self, axis):
        f, t, z, yl, c, yh, x = place()
        self.axis = axis
        if axis == "tp":
            self.k, self.r, self.c = x, yh, 0
            self.dev = lambda r, k: (f, r * 4 + k)
        else:
            self.k, self.r, self.c = z, yl, c
            self.dev = lambda r, k: ((k * 2 + r) * 2 + c, t)
            self.sib = ((z * 2 + yl) * 2 + 1 - c, t)
        self.up, self.down, self.far = lax.rem(self.k + 1, 4), lax.rem(self.k + 3, 4), lax.rem(self.k + 2, 4)
        self.other = 1 - self.r

    def index(self, r, k, c=None):
        if self.axis == "tp":
            return r * 4 + k
        return (k * 2 + r) * 2 + (self.c if c is None else c)


class Mover:
    def __init__(self, group, ssem, rsem):
        self.g, self.ssem, self.rsem, self.plan, self.lands = group, ssem, rsem, {}, {}

    def send(self, *numbers):
        for n in numbers:
            src, dst, to = self.plan[n]
            remote(src, dst, self.ssem.at[n], self.rsem.at[n], to).start()

    def recv(self, *numbers):
        for n in numbers:
            land = self.lands[n]
            remote(land, land, self.ssem.at[n], self.rsem.at[n], self.plan[n][2]).wait_recv()

    def sent(self):
        for n, (src, dst, to) in self.plan.items():
            remote(src, dst, self.ssem.at[n], self.rsem.at[n], to).wait_send()


class Gather(Mover):
    def __init__(self, group, block, half, ssem, rsem, sibling=False):
        super().__init__(group, ssem, rsem)
        g = group
        self.sibling = sibling

        def add(n, src, land, to):
            self.plan[n], self.lands[n] = (src, src, to), land

        add(0, block(g.index(g.r, g.k)), block(g.index(g.other, g.k)), g.dev(g.other, g.k))
        for row, r in enumerate((g.r, g.other)):
            up, down = g.dev(g.r, g.up), g.dev(g.r, g.down)
            here = g.index(r, g.k)
            above, below, far = g.index(r, g.up), g.index(r, g.down), g.index(r, g.far)
            n = 1 + 4 * row
            add(n, half(here, 0), half(below, 0), up)
            add(n + 1, half(here, 1), half(above, 1), down)
            add(n + 2, half(here, 1), half(below, 1), up)
            add(n + 3, half(here, 0), half(above, 0), down)
            add(9 + 2 * row, half(below, 0), half(far, 0), up)
            add(10 + 2 * row, half(above, 1), half(far, 1), down)
        if sibling:
            for row, r in enumerate((g.r, g.other)):
                for j, k in enumerate((g.k, g.down, g.up, g.far)):
                    add(13 + 4 * row + j, block(g.index(r, k)), block(g.index(r, k, 1 - g.c)), g.sib)

    def pass_on(self, *numbers):
        if self.sibling:
            self.send(*numbers)

    def ring(self, row):
        n = 1 + 4 * row
        self.send(n, n + 1, n + 2, n + 3)
        self.pass_on(13 + 4 * row)

    def pair_send(self):
        self.send(0)

    def pair_recv(self):
        self.recv(0)
        self.ring(1)

    def forward(self, row):
        n = 1 + 4 * row
        self.recv(n)
        self.send(9 + 2 * row)
        self.recv(n + 1)
        self.send(10 + 2 * row)

    def near(self, row):
        n = 1 + 4 * row
        self.recv(n + 2, n + 3)
        self.pass_on(14 + 4 * row, 15 + 4 * row)

    def far(self, row):
        self.recv(9 + 2 * row, 10 + 2 * row)
        self.pass_on(16 + 4 * row)

    def finish(self):
        if self.sibling:
            self.recv(*range(13, 21))
        self.sent()


def add_rows(out, ins, chunk):
    @pl.loop(0, out.shape[0] // chunk)
    def _(i):
        rows = pl.ds(pl.multiple_of(i * chunk, chunk), chunk)
        total = ins[0][rows, :].astype(F32)
        for ref in ins[1:]:
            total = total + ref[rows, :].astype(F32)
        out[rows, :] = total.astype(out.dtype)


class Scatter(Mover):
    def __init__(self, group, block, half, far, near, pair, ssem, rsem, chunk, sib=None):
        super().__init__(group, ssem, rsem)
        g = group
        self.block, self.half, self.chunk = block, half, chunk
        self.far_ref, self.near_ref, self.pair_ref, self.sib_ref = far, near, pair, sib
        self.rows = (g.other, g.r)
        self.order = [(g.other, g.far), (g.r, g.far), (g.other, g.up), (g.other, g.down)]
        self.order += [(g.r, g.up), (g.r, g.down), (g.other, g.k), (g.r, g.k)]
        size = near.shape[2] // 2

        def add(n, src, dst, to):
            self.plan[n], self.lands[n] = (src, dst, to), dst

        for row, r in enumerate(self.rows):
            n = 6 * row
            up, down = g.dev(g.r, g.up), g.dev(g.r, g.down)
            above, below, far_at = g.index(r, g.up), g.index(r, g.down), g.index(r, g.far)
            add(n, half(far_at, 0), far.at[row, 0], up)
            add(n + 1, half(far_at, 1), far.at[row, 1], down)
            add(n + 2, half(above, 1), near.at[row, 0, pl.ds(size, size)], up)
            add(n + 3, half(below, 0), near.at[row, 1, pl.ds(0, size)], down)
            add(n + 4, half(above, 0), near.at[row, 0, pl.ds(0, size)], up)
            add(n + 5, half(below, 1), near.at[row, 1, pl.ds(size, size)], down)
        add(12, block(g.index(g.other, g.k)), pair, g.dev(g.other, g.k))
        if sib is not None:
            for s, (r, k) in enumerate(self.order):
                add(13 + s, block(g.index(r, k, 1 - g.c)), sib.at[s], g.sib)

    def chip(self, s):
        r, k = self.order[s]
        return k * 2 + r

    def sib_send(self, s):
        self.send(13 + s)

    def sib_add(self, s):
        self.recv(13 + s)
        mine = self.block(self.g.index(*self.order[s]))
        add_rows(mine, [mine, self.sib_ref.at[s]], self.chunk)

    def far(self, row):
        self.send(6 * row, 6 * row + 1)

    def free(self, row):
        self.send(6 * row + 2, 6 * row + 3)

    def relay(self, row):
        for way, k in ((0, self.g.up), (1, self.g.down)):
            n = 6 * row + way
            self.recv(n)
            mine = self.half(self.g.index(self.rows[row], k), way)
            add_rows(mine, [mine, self.far_ref.at[row, way]], self.chunk)
            self.send(n + 4)

    def pair(self):
        self.recv(2, 3, 4, 5)
        mine = self.block(self.g.index(*self.order[6]))
        add_rows(mine, [mine, self.near_ref.at[0, 0], self.near_ref.at[0, 1]], self.chunk)
        self.send(12)

    def last(self):
        self.recv(8, 9, 10, 11, 12)
        return [self.block(self.g.index(*self.order[7])), self.near_ref.at[1, 0], self.near_ref.at[1, 1], self.pair_ref]


def dot_nn(a, b):
    return jnp.dot(a, b, preferred_element_type=F32)


def dot_nt(a, b):
    return lax.dot_general(a, b, (((1,), (1,)), ((), ())), preferred_element_type=F32)


def dot_tn(a, b):
    return lax.dot_general(a, b, (((0,), (0,)), ((), ())), preferred_element_type=F32)


def rotary_rows():
    lane = np.arange(128) % HD
    freqs = (10000.0 ** (-np.arange(ROT // 2) * 2.0 / ROT)).astype(np.float32)
    angle = np.arange(SEQ_LEN, dtype=np.float32)[:, None] * freqs[lane % (ROT // 2)][None, :]
    turned = lane < ROT
    cos = np.where(turned, np.cos(angle), 1.0)
    sin = np.where(turned, np.sin(angle) * np.where(lane < ROT // 2, -1.0, 1.0), 0.0)
    return np.stack([cos, sin]).astype(np.float32)


def turn(values, cos, sin):
    lane = lax.broadcasted_iota(jnp.int32, values.shape, 1)
    first = lax.rem(lane, HD) < ROT // 2
    partner = jnp.where(first, pltpu.roll(values, 240, 1), pltpu.roll(values, 16, 1))
    return values * cos + partner * sin


def tables(tab, rows):
    cos, sin = tab[0, rows, :], tab[1, rows, :]
    return jnp.concatenate([cos, cos], axis=1), jnp.concatenate([sin, sin], axis=1)


def head_lanes(h, rows):
    lane = lax.broadcasted_iota(jnp.int32, (rows, 256), 1)
    return lax.div(lane, HD) == h


RB = 256


def rows_of(i):
    return pl.ds(pl.multiple_of(i * RB, RB), RB)


def project(i, n, wa, bias, tab, q, k, v, a, dh):
    rows = rows_of(i)
    cos, sin = tables(tab, rows)
    joined = dot_nn(n[rows, :], wa[...]) + bias[0:1, :]
    q[rows, :] = (turn(joined[:, :256], cos, sin) * HD**-0.5).astype(BF16)
    k[rows, :] = turn(joined[:, 256:512], cos, sin).astype(BF16)
    v[rows, :] = joined[:, 512:768].astype(BF16)
    z = joined[:, 768:]
    z2 = z * z
    th = jnp.tanh(z * (GELU + (GELU * 0.044715) * z2))
    half = 0.5 + 0.5 * th
    a[rows, 256:] = (z * half).astype(BF16)
    dh[rows, 768:] = (half + (half - half * half) * z * (2 * GELU + (6 * GELU * 0.044715) * z2)).astype(BF16)


def attend(i, q, k, v, a, lse):
    rows, before = slice(i * RB, (i + 1) * RB), i * RB
    qb = q[rows, :]
    causal = lax.broadcasted_iota(jnp.int32, (RB, RB), 1) <= lax.broadcasted_iota(jnp.int32, (RB, RB), 0)
    lane = lax.broadcasted_iota(jnp.int32, (RB, 128), 1)
    context = jnp.zeros((RB, 256), F32)
    logs = jnp.zeros((RB, 128), F32)
    for h in range(4):
        mine = head_lanes(h, RB)
        qh = jnp.where(mine, qb, jnp.zeros_like(qb))
        s1 = jnp.where(causal, dot_nt(qh, k[rows, :]), -1e30)
        top = jnp.max(s1, axis=1, keepdims=True)
        if i:
            s0 = dot_nt(qh, k[:before, :])
            top = jnp.maximum(top, jnp.max(s0, axis=1, keepdims=True))
        p1 = jnp.exp(s1 - top)
        total = jnp.sum(p1, axis=1, keepdims=True)
        out = dot_nn(p1.astype(BF16), v[rows, :])
        if i:
            p0 = jnp.exp(s0 - top)
            total = total + jnp.sum(p0, axis=1, keepdims=True)
            out = out + dot_nn(p0.astype(BF16), v[:before, :])
        context = jnp.where(mine, out / total, context)
        logs = jnp.where(lane == h, top + jnp.log(total), logs)
    a[rows, :256] = context.astype(BF16)
    lse[rows, :] = logs


def attend_back(i, q, k, v, lse, tab, dh, dk, dv, ps, ds):
    rows, width = slice(i * RB, (i + 1) * RB), (i + 1) * RB
    qb, gb = q[rows, :], dh[rows, :256]
    causal = lax.broadcasted_iota(jnp.int32, (RB, RB), 1) <= lax.broadcasted_iota(jnp.int32, (RB, RB), 0)
    dq = jnp.zeros((RB, 256), F32)
    for h in range(4):
        mine = head_lanes(h, RB)
        part = slice(h * RB, (h + 1) * RB)
        qh = jnp.where(mine, qb, jnp.zeros_like(qb))
        gh = jnp.where(mine, gb, jnp.zeros_like(gb))
        ps[part, SEQ_LEN:] = qh
        ds[part, SEQ_LEN : SEQ_LEN + 256] = gh
        log = lse[rows, h : h + 1]
        s = dot_nt(qh, k[:width, :])
        if i:
            s = jnp.concatenate([s[:, : i * RB], jnp.where(causal, s[:, i * RB :], -1e30)], axis=1)
        else:
            s = jnp.where(causal, s, -1e30)
        p = jnp.exp(s - log)
        t = p * dot_nt(gh, v[:width, :])
        row = jnp.sum(t, axis=1, keepdims=True)
        low = (t - p * row).astype(BF16)
        ps[part, :width] = p.astype(BF16)
        ds[part, :width] = low
        dq = jnp.where(mine, dot_nn(low, k[:width, :]), dq)
    key = dot_tn(ds[:, :width], ps[:, SEQ_LEN:])
    val = dot_tn(ps[:, :width], ds[:, SEQ_LEN : SEQ_LEN + 256])
    if i == 3:
        dk[...] = key
        dv[...] = val
    else:
        dk[:width, :] += key
        dv[:width, :] += val
    cos, sin = tables(tab, rows)
    dh[rows, :256] = turn(dq * HD**-0.5, cos, -sin).astype(BF16)


def keys_back(tab, dh, dk, dv):
    @pl.loop(0, 4)
    def _(i):
        rows = rows_of(i)
        cos, sin = tables(tab, rows)
        dh[rows, 256:512] = turn(dk[rows, :], cos, -sin).astype(BF16)
        dh[rows, 512:768] = dv[rows, :].astype(BF16)


def branch_out(i, a, wb, o):
    rows = rows_of(i)
    o[rows, :] = dot_nn(a[rows, :], wb[...]).astype(BF16)


def branch_back(i, g, wb, dh):
    rows = rows_of(i)
    back = dot_nt(g[rows, :], wb[...])
    dh[rows, :256] = back[:, :256].astype(BF16)
    dh[rows, 768:] = (back[:, 256:] * dh[rows, 768:].astype(F32)).astype(BF16)


def columns_of(m):
    return pl.ds(pl.multiple_of(m * 256, 256), 256)


def grad_wb(m, a, g, wb):
    cols = columns_of(m)
    wb[:, cols] = dot_tn(a[...], g[:, cols]).astype(BF16)


def normed_back(i, dh, wa, out):
    rows = rows_of(i)
    out[rows, :] = dot_nt(dh[rows, :], wa[...]).astype(BF16)


def grad_wa(m, n, dh, wa):
    cols = columns_of(m)
    wa[cols, :] = dot_tn(n[:, cols], dh[...]).astype(BF16)


def grad_bias(dh, put):
    total = jnp.sum(dh[0:RB, :].astype(F32), axis=0, keepdims=True)
    for i in range(1, 4):
        total = total + jnp.sum(dh[i * RB : (i + 1) * RB, :].astype(F32), axis=0, keepdims=True)
    for j in range(WA // 128):
        put(j, total[:, j * 128 : (j + 1) * 128])


def row_block(ref):
    return lambda i: ref.at[pl.ds(pl.multiple_of(i * TOK, TOK), TOK)]


def row_half(ref):
    return lambda i, h: ref.at[pl.ds(pl.multiple_of(i * TOK + h * (TOK // 2), TOK // 2), TOK // 2)]


def col_block(ref):
    return lambda i: ref.at[:, pl.ds(pl.multiple_of(i * 128, 128), 128)]


def col_half(ref):
    return lambda i, h: ref.at[pl.ds(h * (WB // 2), WB // 2), pl.ds(pl.multiple_of(i * 128, 128), 128)]


def sixteen_rows(i):
    return pl.ds(pl.multiple_of(i * 16, 16), 16)


def load_rows(src, dst, sem):
    copies = [pltpu.make_async_copy(src.at[pl.ds(j * 64, 64)], dst.at[j], sem.at[j]) for j in range(2)]
    for copy in copies:
        copy.start()
    return copies


def loaded(ref, i):
    return ref[lax.div(i, 4), pl.ds(pl.multiple_of(lax.rem(i, 4) * 16, 16), 16), :].astype(F32)


def block_kernel(x_ref, cot_ref, gain_ref, shift_ref, dense_b, down_b, qkv_ref, up_ref, dense_ref, down_ref, qkv_b, up_b, tab_ref,
                 out_ref, ig_ref, vec_out, dqkv_out, dup_out, ddense_out, ddown_out, db_out, xhats,
                 n, g, wa, wb, vecs, bias, o, q, k, v, a, dh, lse, dk, dv, tab,
                 sib_a, sib_b, far_a, near_a, pair_a, far_b, near_b, pair_b, far_o, near_o, pair_o, far_n, near_n, pair_n,
                 part, v1, v2, dbs, ssem, rsem, v0s, v0r, v1s, v1r, v2s, v2r, dss, dsr, lsem):
    f, t = lax.axis_index("fsdp"), lax.axis_index("tp")
    tp, fs = Group("tp"), Group("fsdp")
    wa_own, wb_own = row_block(wa)(f), col_block(wb)(f)
    vec_slot = col_block(vecs)
    own = [pltpu.make_async_copy(x_ref, row_block(o)(t), lsem.at[0])]
    for j in range(3):
        own.append(pltpu.make_async_copy(qkv_ref.at[j], wa_own.at[:, pl.ds(j * 256, 256)], lsem.at[1 + j]))
    own += [
        pltpu.make_async_copy(up_ref, wa_own.at[:, pl.ds(768, 1024)], lsem.at[4]),
        pltpu.make_async_copy(dense_ref, wb_own.at[pl.ds(0, 256)], lsem.at[5]),
        pltpu.make_async_copy(down_ref, wb_own.at[pl.ds(256, 1024)], lsem.at[6]),
        pltpu.make_async_copy(cot_ref, row_block(g)(t), lsem.at[7]),
        pltpu.make_async_copy(tab_ref, tab, lsem.at[8]),
    ]
    for copy in own:
        copy.start()
    f32_row = lambda ref: ref[...].astype(F32).reshape(1, ref.shape[0])
    rows = [f32_row(gain_ref), f32_row(shift_ref), f32_row(dense_b) + f32_row(down_b), jnp.zeros((5, 128), F32)]
    vecs[:, pl.ds(pl.multiple_of(f * 128, 128), 128)] = jnp.concatenate(rows, axis=0)
    for j in range(3):
        bias[0:1, j * 256 : (j + 1) * 256] = qkv_b[j : j + 1, :].astype(F32)
    bias[0:1, 768:] = f32_row(up_b)
    ga = Gather(fs, row_block(wa), row_half(wa), ssem.at[0], rsem.at[0], sibling=True)
    gb = Gather(fs, col_block(wb), col_half(wb), ssem.at[1], rsem.at[1], sibling=True)
    gn = Gather(tp, row_block(o), row_half(o), ssem.at[2], rsem.at[2])
    gg = Gather(tp, row_block(g), row_half(g), ssem.at[3], rsem.at[3])
    so = Scatter(tp, row_block(o), row_half(o), far_o, near_o, pair_o, ssem.at[4], rsem.at[4], 16)
    sn = Scatter(tp, row_block(g), row_half(g), far_n, near_n, pair_n, ssem.at[5], rsem.at[5], 16)
    sa = Scatter(fs, row_block(wa), row_half(wa), far_a, near_a, pair_a, ssem.at[6], rsem.at[6], 16, sib_a)
    sb = Scatter(fs, col_block(wb), col_half(wb), far_b, near_b, pair_b, ssem.at[7], rsem.at[7], 128, sib_b)

    def normalize(r, k):
        block = r * 4 + k
        parked = (near_o if r is tp.r else near_n).at[lax.div(k, 2), lax.rem(k, 2)]

        @pl.loop(0, 2)
        def _(i):
            rows = pl.ds(pl.multiple_of(block * TOK + i * 64, 64), 64)
            xf = o[rows, :].astype(F32)
            centered = xf - jnp.mean(xf, axis=-1, keepdims=True)
            variance = jnp.mean(centered * centered, axis=-1, keepdims=True)
            xhat = centered * lax.rsqrt(variance + EPS)
            n[rows, :] = (xhat * vecs[0:1, :] + vecs[1:2, :]).astype(BF16)
            parked[pl.ds(pl.multiple_of(i * 64, 64), 64), :] = xhat.astype(BF16)

    greet(all_peers(f, t))
    own[0].wait()
    gn.ring(0)
    for d in range(1, 16):
        remote(vec_slot(f), vec_slot(f), v0s.at[d], v0r.at[d], (lax.rem(f + d, 16), t)).start()
    gn.pair_send()
    for copy in own[1:5]:
        copy.wait()
    ga.ring(0)
    for copy in own[5:]:
        copy.wait()
    gn.forward(0)
    for d in range(1, 16):
        source = lax.rem(f + 16 - d, 16)
        remote(vec_slot(source), vec_slot(source), v0s.at[d], v0r.at[d], (source, t)).wait_recv()
    normalize(tp.r, tp.k)
    ga.forward(0)
    gb.ring(0)
    gn.pair_recv()
    ga.pair_send()
    ga.near(0)
    normalize(tp.other, tp.k)
    gn.near(0)
    normalize(tp.r, tp.down)
    normalize(tp.r, tp.up)
    gb.forward(0)
    ga.pair_recv()
    gb.pair_send()
    gg.pair_send()
    gn.forward(1)
    gn.far(0)
    gg.ring(0)
    part[...] = jnp.zeros_like(part)

    @pl.loop(0, TOK // 16)
    def _(i):
        cot = g[pl.ds(pl.multiple_of(t * TOK + i * 16, 16), 16), :].astype(F32)
        part[16:24, :] += cot[:8] + cot[8:]

    normalize(tp.r, tp.far)
    ga.far(0)
    ga.forward(1)
    gn.near(1)
    normalize(tp.other, tp.down)
    normalize(tp.other, tp.up)
    gb.near(0)
    gb.pair_recv()
    ga.near(1)
    gn.far(1)
    normalize(tp.other, tp.far)
    keep = [pltpu.make_async_copy(ref, xhats.at[i], lsem.at[9 + i]) for i, ref in enumerate((near_o, near_n))]
    for copy in keep:
        copy.start()
    ga.far(1)
    ga.finish()
    project(0, n, wa, bias, tab, q, k, v, a, dh)
    gg.forward(0)
    gb.far(0)
    gb.forward(1)
    project(1, n, wa, bias, tab, q, k, v, a, dh)
    gg.pair_recv()
    project(2, n, wa, bias, tab, q, k, v, a, dh)
    gb.near(1)
    project(3, n, wa, bias, tab, q, k, v, a, dh)
    gn.sent()
    attend(0, q, k, v, a, lse)
    attend(1, q, k, v, a, lse)
    gg.near(0)
    gb.far(1)
    attend(2, q, k, v, a, lse)
    attend(3, q, k, v, a, lse)
    gb.finish()
    side = lax.div(tp.far, 2)
    halves = (tp.other * 2 + side, tp.r * 2 + side, tp.other * 2 + 1 - side, tp.r * 2 + 1 - side)
    for copy in keep:
        copy.wait()
    branch_out(halves[0], a, wb, o)
    gg.forward(1)

    @pl.loop(1, 4)
    def _(i):
        step = jnp.where(i == 1, halves[1], jnp.where(i == 2, halves[2], halves[3]))
        branch_out(step, a, wb, o)

    gg.far(0)
    branch_back(tp.r * 2, g, wb, dh)
    branch_back(tp.r * 2 + 1, g, wb, dh)
    gg.near(1)
    gg.far(1)
    so.far(0)
    so.far(1)
    gg.finish()
    branch_back(tp.other * 2, g, wb, dh)
    branch_back(tp.other * 2 + 1, g, wb, dh)
    so.free(0)
    for s in range(8):
        grad_wb(sb.chip(s), a, g, wb)
        sb.sib_send(s)
        if s > 1:
            sb.sib_add(s - 2)
        if s == 2:
            sb.far(0)
        if s == 3:
            sb.far(1)
        if s == 4:
            so.relay(0)
            so.free(1)
        if s == 5:
            sb.free(0)
    sb.sib_add(6)
    sb.sib_add(7)
    sb.free(1)
    so.relay(1)
    for i in (3, 2, 1, 0):
        attend_back(i, q, k, v, lse, tab, dh, dk, dv, a, g)
        if i == 3:
            sb.relay(0)
        if i == 2:
            sb.relay(1)

    def fetch(j):
        place, sem = (j % 2) * 2 * RB, (j % 2) * 4
        src = xhats.at[1 - j % 2, side if j < 2 else 1 - side]
        copies = []
        for half in range(2):
            for i in range(2):
                dst = a.at[pl.ds(place + half * RB + i * TOK, TOK), pl.ds(0, 1024)]
                piece_in = src.at[i, :, pl.ds(half * 1024, 1024)]
                copies.append(pltpu.make_async_copy(piece_in, dst, lsem.at[29 + sem + half * 2 + i]))
        for copy in copies:
            copy.start()
        return copies

    def norm_sums(j):
        place, first = (j % 2) * 2 * RB, halves[j] * RB

        @pl.loop(0, RB // 64)
        def _(i):
            rows = pl.ds(pl.multiple_of(first + i * 64, 64), 64)
            for half in range(2):
                cols = slice(half * 1024, half * 1024 + 1024)
                grad = g[rows, cols].astype(F32)
                xhat = a[pl.ds(pl.multiple_of(place + half * RB + i * 64, 64), 64), 0:1024].astype(F32)
                part[0:8, cols] += jnp.sum((grad * xhat).reshape(8, 8, 1024), axis=0)
                part[8:16, cols] += jnp.sum(grad.reshape(8, 8, 1024), axis=0)

    fetched = [fetch(0), fetch(1)]
    keys_back(tab, dh, dk, dv)
    for j in range(4):
        normed_back(halves[j], dh, wa, g)
        if j < 2:
            sn.far(j)
        for copy in fetched[j]:
            copy.wait()
        norm_sums(j)
        if j < 2:
            fetched.append(fetch(j + 2))
        if j == 1:
            so.pair()
            sb.pair()
    sn.free(0)
    for row in range(3):
        part[24 + row : 25 + row, :] = jnp.sum(part[row * 8 : row * 8 + 8, :], axis=0, keepdims=True)
    piece = lambda i: part.at[pl.ds(24, 8), pl.ds(pl.multiple_of(i * 128, 128), 128)]
    for d in range(1, 16):
        to = lax.rem(f + d, 16)
        remote(piece(to), v1.at[f], v1s.at[d], v1r.at[d], (to, t)).start()
    v1[f] = part[24:, pl.ds(pl.multiple_of(f * 128, 128), 128)]

    for s in range(8):
        grad_wa(sa.chip(s), n, dh, wa)
        sa.sib_send(s)
        if s > 1:
            sa.sib_add(s - 2)
        if s == 2:
            sa.far(0)
        if s == 3:
            sa.far(1)
            sn.relay(0)
            sn.free(1)
        if s == 5:
            sa.free(0)
    sa.sib_add(6)
    sa.sib_add(7)
    sa.free(1)

    def put(j, row):
        dbs[f, j : j + 1, :] = row

    grad_bias(dh, put)
    dbs[f, WA // 128 :, :] = jnp.zeros((16 - WA // 128, 128), F32)
    for d in range(1, 16):
        remote(dbs.at[f], dbs.at[f], dss.at[d], dsr.at[d], (lax.rem(f + d, 16), t)).start()
    for d in range(1, 16):
        source = lax.rem(f + 16 - d, 16)
        remote(piece(source), v1.at[source], v1s.at[d], v1r.at[d], (source, t)).wait_recv()
    v2[t] = jnp.sum(v1[...], axis=0)
    for d in range(1, 8):
        remote(v2.at[t], v2.at[t], v2s.at[d], v2r.at[d], (f, lax.rem(t + d, 8))).start()
    sn.relay(1)
    sa.relay(0)
    out_refs = so.last()
    rows_in = load_rows(x_ref, far_o.at[1], lsem.at[pl.ds(27, 2)])
    for copy in rows_in:
        copy.wait()

    @pl.loop(0, TOK // 16)
    def _(i):
        rows = sixteen_rows(i)
        total = loaded(far_o.at[1], i) + vecs[2:3, :]
        for ref in out_refs:
            total = total + ref[rows, :].astype(F32)
        pair_o[rows, :] = total.astype(BF16)

    results = [pltpu.make_async_copy(pair_o, out_ref, lsem.at[14])]
    results[0].start()
    cots = load_rows(cot_ref, far_o.at[0], lsem.at[pl.ds(25, 2)])

    sa.relay(1)
    sb_refs = sb.last()
    dense_sum, down_sum = dk.at[pl.ds(0, 256), pl.ds(128, 128)], dk.at[:, pl.ds(0, 128)]
    add_rows(dense_sum, [ref.at[pl.ds(0, 256)] for ref in sb_refs], 128)
    add_rows(down_sum, [ref.at[pl.ds(256, 1024)] for ref in sb_refs], 128)
    results.append(pltpu.make_async_copy(dense_sum, ddense_out, lsem.at[15]))
    results.append(pltpu.make_async_copy(down_sum, ddown_out, lsem.at[16]))
    results[1].start()
    results[2].start()
    sn.pair()
    sa.pair()
    for d in range(1, 16):
        source = lax.rem(f + 16 - d, 16)
        remote(dbs.at[source], dbs.at[source], dss.at[d], dsr.at[d], (source, t)).wait_recv()
    db_out[...] = jnp.sum(dbs[...], axis=0)
    for d in range(1, 8):
        source = lax.rem(t + 8 - d, 8)
        remote(v2.at[source], v2.at[source], v2s.at[d], v2r.at[d], (f, source)).wait_recv()
    vec_out[...] = jnp.sum(v2[...], axis=0)
    for copy in cots:
        copy.wait()
    n_refs = sn.last()

    @pl.loop(0, 2)
    def _(i):
        rows = pl.ds(pl.multiple_of(i * 64, 64), 64)
        xf = far_o[1, i].astype(F32)
        centered = xf - jnp.mean(xf, axis=-1, keepdims=True)
        inv = lax.rsqrt(jnp.mean(centered * centered, axis=-1, keepdims=True) + EPS)
        xhat = centered * inv
        total = n_refs[0][rows, :].astype(F32)
        for ref in n_refs[1:]:
            total = total + ref[rows, :].astype(F32)
        e = total * vecs[0:1, :]
        back = (e - jnp.mean(e, axis=-1, keepdims=True) - xhat * jnp.mean(e * xhat, axis=-1, keepdims=True)) * inv
        pair_n[rows, :] = (far_o[0, i].astype(F32) + back).astype(BF16)

    results.append(pltpu.make_async_copy(pair_n, ig_ref, lsem.at[17]))
    results[3].start()
    sa_refs = sa.last()
    for j in range(7):
        here = dv.at[pl.ds(j * TOK, TOK)]
        add_rows(here, [ref.at[:, pl.ds(j * 256, 256)] for ref in sa_refs], TOK)
        there = dqkv_out.at[j] if j < 3 else dup_out.at[:, pl.ds((j - 3) * 256, 256)]
        results.append(pltpu.make_async_copy(here, there, lsem.at[18 + j]))
        results[-1].start()
    for copy in results:
        copy.wait()
    for op in (so, sn, sa, sb):
        op.sent()
    for d in range(1, 16):
        to = lax.rem(f + d, 16)
        remote(vec_slot(f), vec_slot(f), v0s.at[d], v0r.at[d], (to, t)).wait_send()
        remote(dbs.at[f], dbs.at[f], dss.at[d], dsr.at[d], (to, t)).wait_send()
        remote(piece(to), v1.at[f], v1s.at[d], v1r.at[d], (to, t)).wait_send()
    for d in range(1, 8):
        remote(v2.at[t], v2.at[t], v2s.at[d], v2r.at[d], (f, lax.rem(t + d, 8))).wait_send()


def run_block(*operands):
    def bufs(full, half):
        return [pltpu.VMEM((2, 2) + half, BF16), pltpu.VMEM((2, 2) + full, BF16), pltpu.VMEM(full, BF16)]

    dma = pltpu.SemaphoreType.DMA
    sds = jax.ShapeDtypeStruct
    return pl.pallas_call(
        block_kernel,
        out_shape=(
            sds((TOK, D), BF16),
            sds((TOK, D), BF16),
            sds((8, 128), F32),
            sds((3, TOK, 256), F32),
            sds((TOK, 1024), F32),
            sds((256, 128), F32),
            sds((1024, 128), F32),
            sds((16, 128), F32),
            sds((2, 2, 2, TOK, D), BF16),
        ),
        in_specs=[ANY, ANY, VMEM, VMEM, VMEM, VMEM, ANY, ANY, ANY, ANY, VMEM, VMEM, ANY],
        out_specs=(ANY, ANY, VMEM, ANY, ANY, ANY, ANY, VMEM, ANY),
        scratch_shapes=[
            pltpu.VMEM((SEQ_LEN, D), BF16),
            pltpu.VMEM((SEQ_LEN, D), BF16),
            pltpu.VMEM((D, WA), BF16),
            pltpu.VMEM((WB, D), BF16),
            pltpu.VMEM((8, D), F32),
            pltpu.VMEM((1, WA), F32),
            pltpu.VMEM((SEQ_LEN, D), BF16),
            pltpu.VMEM((SEQ_LEN, 256), BF16),
            pltpu.VMEM((SEQ_LEN, 256), BF16),
            pltpu.VMEM((SEQ_LEN, 256), BF16),
            pltpu.VMEM((SEQ_LEN, WB), BF16),
            pltpu.VMEM((SEQ_LEN, WA), BF16),
            pltpu.VMEM((SEQ_LEN, 128), F32),
            pltpu.VMEM((SEQ_LEN, 256), F32),
            pltpu.VMEM((SEQ_LEN, 256), F32),
            pltpu.VMEM((2, SEQ_LEN, 128), F32),
            pltpu.VMEM((8, TOK, WA), BF16),
            pltpu.VMEM((8, WB, 128), BF16),
            *bufs((TOK, WA), (TOK // 2, WA)),
            *bufs((WB, 128), (WB // 2, 128)),
            *bufs((TOK, D), (TOK // 2, D)),
            *bufs((TOK, D), (TOK // 2, D)),
            pltpu.VMEM((32, D), F32),
            pltpu.VMEM((16, 8, 128), F32),
            pltpu.VMEM((8, 8, 128), F32),
            pltpu.VMEM((16, 16, 128), F32),
            dma((8, 21)), dma((8, 21)),
            dma((16,)), dma((16,)), dma((16,)), dma((16,)), dma((8,)), dma((8,)), dma((16,)), dma((16,)), dma((37,)),
        ],
        compiler_params=pltpu.CompilerParams(collective_id=0, has_side_effects=True, vmem_limit_bytes=64 * 2**20 - 2**18),
        name="block_all",
    )(*operands)


def give_kernel(out_in, ig_in, dqkv_in, dup_in, ddense_in, ddown_in, vec, db,
                out, ig, gain, shift, dqkv, qkv_b, ddense, dense_b, dup, up_b, ddown, down_b, sem):
    pairs = [(out_in, out), (ig_in, ig), (dqkv_in, dqkv), (dup_in, dup), (ddense_in, ddense), (ddown_in, ddown)]
    copies = [pltpu.make_async_copy(src, dst, sem.at[i]) for i, (src, dst) in enumerate(pairs)]
    for copy in copies:
        copy.start()
    gain[...] = vec[0, :]
    shift[...] = vec[1, :]
    dense_b[...] = vec[2, :]
    down_b[...] = vec[2, :]
    for j in range(6):
        qkv_b[j // 2 : j // 2 + 1, (j % 2) * 128 : (j % 2) * 128 + 128] = db[j : j + 1, :]
    for j in range(8):
        up_b[pl.ds(j * 128, 128)] = db[6 + j, :]
    for copy in copies:
        copy.wait()


def give(*results):
    sds = jax.ShapeDtypeStruct
    return pl.pallas_call(
        give_kernel,
        out_shape=(
            sds((TOK, D), BF16),
            sds((TOK, D), BF16),
            sds((128,), F32),
            sds((128,), F32),
            sds((3, TOK, 256), F32),
            sds((3, 256), F32),
            sds((256, 128), F32),
            sds((128,), F32),
            sds((TOK, 1024), F32),
            sds((1024,), F32),
            sds((1024, 128), F32),
            sds((128,), F32),
        ),
        in_specs=[VMEM] * 8,
        out_specs=(ANY, ANY, VMEM, VMEM, ANY, VMEM, ANY, VMEM, ANY, VMEM, ANY, VMEM),
        scratch_shapes=[pltpu.SemaphoreType.DMA((6,))],
        compiler_params=pltpu.CompilerParams(vmem_limit_bytes=60 * 2**20),
        name="give",
    )(*results)


def on_device(
    block_input, norm_gain, norm_bias, qkv_weight, qkv_bias, dense_weight, dense_bias, up_weight, up_bias,
    down_weight, down_bias, cotangent,
):
    out, ig, vec, dqkv, dup, ddense, ddown, db, _ = run_block(
        block_input, cotangent, norm_gain, norm_bias, dense_bias, down_bias, jnp.transpose(qkv_weight, (1, 0, 2)),
        up_weight, dense_weight, down_weight, qkv_bias, up_bias, jnp.asarray(rotary_rows()),
    )
    results = list(give(out, ig, dqkv, dup, ddense, ddown, vec, db))
    results[4] = jnp.transpose(results[4], (1, 0, 2))
    return tuple(results)


def solution(mesh):
    in_specs = (
        P(("fsdp", "tp"), None),
        P("fsdp"),
        P("fsdp"),
        P("fsdp", None, "tp"),
        P(None, "tp"),
        P("tp", "fsdp"),
        P("fsdp"),
        P("fsdp", "tp"),
        P("tp"),
        P("tp", "fsdp"),
        P("fsdp"),
        P(("fsdp", "tp"), None),
    )
    out_specs = (
        P(("fsdp", "tp"), None),
        P(("fsdp", "tp"), None),
        P("fsdp"),
        P("fsdp"),
        P("fsdp", None, "tp"),
        P(None, "tp"),
        P("tp", "fsdp"),
        P("fsdp"),
        P("fsdp", "tp"),
        P("tp"),
        P("tp", "fsdp"),
        P("fsdp"),
    )
    return jax.shard_map(
        on_device, mesh=mesh, in_specs=in_specs, out_specs=out_specs, check_vma=False
    )
```

```python
import jax
import jax.numpy as jnp
import numpy as np
from jax import lax
from jax.experimental import pallas as pl
from jax.experimental.pallas import tpu as pltpu
from jax.sharding import PartitionSpec as P

HD = 64
ROT = 32
SEQ_LEN = 1024
EPS = 1e-05
D = 2048
TOK = 128
WA = 1792
WB = 1280
GELU = 0.7978845608028654
F32 = jnp.float32
BF16 = jnp.bfloat16
MESH = pl.DeviceIdType.MESH
ANY = pl.BlockSpec(memory_space=pl.ANY)
VMEM = pl.BlockSpec(memory_space=pltpu.VMEM)


def place():
    f = lax.axis_index("fsdp")
    t = lax.axis_index("tp")
    return f, t, lax.div(f, 4), lax.rem(lax.div(f, 2), 2), lax.rem(f, 2), lax.div(t, 4), lax.rem(t, 4)


def greet(peers):
    barrier = pltpu.get_barrier_semaphore()
    for peer in peers:
        pl.semaphore_signal(barrier, inc=1, device_id=peer, device_id_type=MESH)
    pl.semaphore_wait(barrier, len(peers))


def all_peers(f, t):
    peers = [(lax.rem(f + d, 16), t) for d in range(1, 16)]
    return peers + [(f, lax.rem(t + d, 8)) for d in range(1, 8)]


def remote(src, dst, ssem, rsem, to):
    return pltpu.make_async_remote_copy(
        src_ref=src, dst_ref=dst, send_sem=ssem, recv_sem=rsem, device_id=to, device_id_type=MESH
    )


class Group:
    def __init__(self, axis):
        f, t, z, yl, c, yh, x = place()
        self.axis = axis
        if axis == "tp":
            self.k, self.r, self.c = x, yh, 0
            self.dev = lambda r, k: (f, r * 4 + k)
        else:
            self.k, self.r, self.c = z, yl, c
            self.dev = lambda r, k: ((k * 2 + r) * 2 + c, t)
            self.sib = ((z * 2 + yl) * 2 + 1 - c, t)
        self.up, self.down, self.far = lax.rem(self.k + 1, 4), lax.rem(self.k + 3, 4), lax.rem(self.k + 2, 4)
        self.other = 1 - self.r

    def index(self, r, k, c=None):
        if self.axis == "tp":
            return r * 4 + k
        return (k * 2 + r) * 2 + (self.c if c is None else c)


class Mover:
    def __init__(self, group, ssem, rsem):
        self.g, self.ssem, self.rsem, self.plan, self.lands = group, ssem, rsem, {}, {}

    def send(self, *numbers):
        for n in numbers:
            src, dst, to = self.plan[n]
            remote(src, dst, self.ssem.at[n], self.rsem.at[n], to).start()

    def recv(self, *numbers):
        for n in numbers:
            land = self.lands[n]
            remote(land, land, self.ssem.at[n], self.rsem.at[n], self.plan[n][2]).wait_recv()

    def sent(self):
        for n, (src, dst, to) in self.plan.items():
            remote(src, dst, self.ssem.at[n], self.rsem.at[n], to).wait_send()


class Gather(Mover):
    def __init__(self, group, block, half, ssem, rsem, sibling=False):
        super().__init__(group, ssem, rsem)
        g = group
        self.sibling = sibling

        def add(n, src, land, to):
            self.plan[n], self.lands[n] = (src, src, to), land

        add(0, block(g.index(g.r, g.k)), block(g.index(g.other, g.k)), g.dev(g.other, g.k))
        for row, r in enumerate((g.r, g.other)):
            up, down = g.dev(g.r, g.up), g.dev(g.r, g.down)
            here = g.index(r, g.k)
            above, below, far = g.index(r, g.up), g.index(r, g.down), g.index(r, g.far)
            n = 1 + 4 * row
            add(n, half(here, 0), half(below, 0), up)
            add(n + 1, half(here, 1), half(above, 1), down)
            add(n + 2, half(here, 1), half(below, 1), up)
            add(n + 3, half(here, 0), half(above, 0), down)
            add(9 + 2 * row, half(below, 0), half(far, 0), up)
            add(10 + 2 * row, half(above, 1), half(far, 1), down)
        if sibling:
            for row, r in enumerate((g.r, g.other)):
                for j, k in enumerate((g.k, g.down, g.up, g.far)):
                    add(13 + 4 * row + j, block(g.index(r, k)), block(g.index(r, k, 1 - g.c)), g.sib)

    def pass_on(self, *numbers):
        if self.sibling:
            self.send(*numbers)

    def ring(self, row):
        n = 1 + 4 * row
        self.send(n, n + 1, n + 2, n + 3)
        self.pass_on(13 + 4 * row)

    def pair_send(self):
        self.send(0)

    def pair_recv(self):
        self.recv(0)
        self.ring(1)

    def forward(self, row):
        n = 1 + 4 * row
        self.recv(n)
        self.send(9 + 2 * row)
        self.recv(n + 1)
        self.send(10 + 2 * row)

    def near(self, row):
        n = 1 + 4 * row
        self.recv(n + 2, n + 3)
        self.pass_on(14 + 4 * row, 15 + 4 * row)

    def far(self, row):
        self.recv(9 + 2 * row, 10 + 2 * row)
        self.pass_on(16 + 4 * row)

    def finish(self):
        if self.sibling:
            self.recv(*range(13, 21))
        self.sent()


def pick(i, values):
    out = values[0]
    for j, value in enumerate(values[1:], 1):
        out = jnp.where(i == j, value, out)
    return out


def add_rows(out, ins, chunk):
    @pl.loop(0, out.shape[0] // chunk)
    def _(i):
        rows = pl.ds(pl.multiple_of(i * chunk, chunk), chunk)
        total = ins[0][rows, :].astype(F32)
        for ref in ins[1:]:
            total = total + ref[rows, :].astype(F32)
        out[rows, :] = total.astype(out.dtype)


class Scatter(Mover):
    def __init__(self, group, block, half, far, near, pair, ssem, rsem, chunk, sib=None):
        super().__init__(group, ssem, rsem)
        g = group
        self.block, self.half, self.chunk = block, half, chunk
        self.far_ref, self.near_ref, self.pair_ref, self.sib_ref = far, near, pair, sib
        self.rows = (g.other, g.r)
        self.order = [(g.other, g.far), (g.r, g.far), (g.other, g.up), (g.other, g.down)]
        self.order += [(g.r, g.up), (g.r, g.down), (g.other, g.k), (g.r, g.k)]
        size = near.shape[2] // 2

        def add(n, src, dst, to):
            self.plan[n], self.lands[n] = (src, dst, to), dst

        for row, r in enumerate(self.rows):
            n = 6 * row
            up, down = g.dev(g.r, g.up), g.dev(g.r, g.down)
            above, below, far_at = g.index(r, g.up), g.index(r, g.down), g.index(r, g.far)
            add(n, half(far_at, 0), far.at[row, 0], up)
            add(n + 1, half(far_at, 1), far.at[row, 1], down)
            add(n + 2, half(above, 1), near.at[row, 0, pl.ds(size, size)], up)
            add(n + 3, half(below, 0), near.at[row, 1, pl.ds(0, size)], down)
            add(n + 4, half(above, 0), near.at[row, 0, pl.ds(0, size)], up)
            add(n + 5, half(below, 1), near.at[row, 1, pl.ds(size, size)], down)
        add(12, block(g.index(g.other, g.k)), pair, g.dev(g.other, g.k))
        if sib is not None:
            for s, (r, k) in enumerate(self.order):
                add(13 + s, block(g.index(r, k, 1 - g.c)), sib.at[s], g.sib)

    def chip(self, s):
        return pick(s, [k * 2 + r for r, k in self.order])

    def sib_copy(self, s):
        src, dst = self.block(self.chip(s) * 2 + 1 - self.g.c), self.sib_ref.at[s]
        return remote(src, dst, self.ssem.at[13 + s], self.rsem.at[13 + s], self.g.sib)

    def sib_add(self, s):
        self.sib_copy(s).wait_recv()
        mine = self.block(self.chip(s) * 2 + self.g.c)
        add_rows(mine, [mine, self.sib_ref.at[s]], self.chunk)

    def far(self, row):
        self.send(6 * row, 6 * row + 1)

    def free(self, row):
        self.send(6 * row + 2, 6 * row + 3)

    def relay(self, row):
        for way, k in ((0, self.g.up), (1, self.g.down)):
            n = 6 * row + way
            self.recv(n)
            mine = self.half(self.g.index(self.rows[row], k), way)
            add_rows(mine, [mine, self.far_ref.at[row, way]], self.chunk)
            self.send(n + 4)

    def pair(self):
        self.recv(2, 3, 4, 5)
        mine = self.block(self.g.index(*self.order[6]))
        add_rows(mine, [mine, self.near_ref.at[0, 0], self.near_ref.at[0, 1]], self.chunk)
        self.send(12)

    def last(self):
        self.recv(8, 9, 10, 11, 12)
        return [self.block(self.g.index(*self.order[7])), self.near_ref.at[1, 0], self.near_ref.at[1, 1], self.pair_ref]


def dot_nn(a, b):
    return jnp.dot(a, b, preferred_element_type=F32)


def dot_nt(a, b):
    return lax.dot_general(a, b, (((1,), (1,)), ((), ())), preferred_element_type=F32)


def dot_tn(a, b):
    return lax.dot_general(a, b, (((0,), (0,)), ((), ())), preferred_element_type=F32)


def rotary_rows():
    lane = np.arange(128) % HD
    freqs = (10000.0 ** (-np.arange(ROT // 2) * 2.0 / ROT)).astype(np.float32)
    angle = np.arange(SEQ_LEN, dtype=np.float32)[:, None] * freqs[lane % (ROT // 2)][None, :]
    turned = lane < ROT
    cos = np.where(turned, np.cos(angle), 1.0)
    sin = np.where(turned, np.sin(angle) * np.where(lane < ROT // 2, -1.0, 1.0), 0.0)
    return np.stack([cos, sin]).astype(np.float32)


def turn(values, cos, sin):
    lane = lax.broadcasted_iota(jnp.int32, values.shape, 1)
    first = lax.rem(lane, HD) < ROT // 2
    partner = jnp.where(first, pltpu.roll(values, 240, 1), pltpu.roll(values, 16, 1))
    return values * cos + partner * sin


def tables(tab, rows):
    cos, sin = tab[0, rows, :], tab[1, rows, :]
    return jnp.concatenate([cos, cos], axis=1), jnp.concatenate([sin, sin], axis=1)


def head_lanes(h, rows):
    lane = lax.broadcasted_iota(jnp.int32, (rows, 256), 1)
    return lax.div(lane, HD) == h


RB = 256


def rows_of(i):
    return pl.ds(pl.multiple_of(i * RB, RB), RB)


def project(i, n, wa, bias, tab, q, k, v, a, dh):
    rows = rows_of(i)
    cos, sin = tables(tab, rows)
    joined = dot_nn(n[rows, :], wa[...]) + bias[0:1, :]
    q[rows, :] = (turn(joined[:, :256], cos, sin) * HD**-0.5).astype(BF16)
    k[rows, :] = turn(joined[:, 256:512], cos, sin).astype(BF16)
    v[rows, :] = joined[:, 512:768].astype(BF16)
    z = joined[:, 768:]
    z2 = z * z
    th = jnp.tanh(z * (GELU + (GELU * 0.044715) * z2))
    half = 0.5 + 0.5 * th
    a[rows, 256:] = (z * half).astype(BF16)
    dh[rows, 768:] = (half + (half - half * half) * z * (2 * GELU + (6 * GELU * 0.044715) * z2)).astype(BF16)


def attend(i, q, k, v, a, lse):
    rows, before = slice(i * RB, (i + 1) * RB), i * RB
    qb = q[rows, :]
    causal = lax.broadcasted_iota(jnp.int32, (RB, RB), 1) <= lax.broadcasted_iota(jnp.int32, (RB, RB), 0)
    lane = lax.broadcasted_iota(jnp.int32, (RB, 128), 1)
    context = jnp.zeros((RB, 256), F32)
    logs = jnp.zeros((RB, 128), F32)
    for h in range(4):
        mine = head_lanes(h, RB)
        qh = jnp.where(mine, qb, jnp.zeros_like(qb))
        s1 = jnp.where(causal, dot_nt(qh, k[rows, :]), -1e30)
        top = jnp.max(s1, axis=1, keepdims=True)
        if i:
            s0 = dot_nt(qh, k[:before, :])
            top = jnp.maximum(top, jnp.max(s0, axis=1, keepdims=True))
        p1 = jnp.exp(s1 - top)
        total = jnp.sum(p1, axis=1, keepdims=True)
        out = dot_nn(p1.astype(BF16), v[rows, :])
        if i:
            p0 = jnp.exp(s0 - top)
            total = total + jnp.sum(p0, axis=1, keepdims=True)
            out = out + dot_nn(p0.astype(BF16), v[:before, :])
        context = jnp.where(mine, out / total, context)
        logs = jnp.where(lane == h, top + jnp.log(total), logs)
    a[rows, :256] = context.astype(BF16)
    lse[rows, :] = logs


def attend_back(i, q, k, v, lse, tab, dh, dk, dv, ps, ds):
    rows, width = slice(i * RB, (i + 1) * RB), (i + 1) * RB
    qb, gb = q[rows, :], dh[rows, :256]
    causal = lax.broadcasted_iota(jnp.int32, (RB, RB), 1) <= lax.broadcasted_iota(jnp.int32, (RB, RB), 0)
    dq = jnp.zeros((RB, 256), F32)
    for h in range(4):
        mine = head_lanes(h, RB)
        part = slice(h * RB, (h + 1) * RB)
        qh = jnp.where(mine, qb, jnp.zeros_like(qb))
        gh = jnp.where(mine, gb, jnp.zeros_like(gb))
        ps[part, SEQ_LEN:] = qh
        ds[part, SEQ_LEN : SEQ_LEN + 256] = gh
        log = lse[rows, h : h + 1]
        s = dot_nt(qh, k[:width, :])
        if i:
            s = jnp.concatenate([s[:, : i * RB], jnp.where(causal, s[:, i * RB :], -1e30)], axis=1)
        else:
            s = jnp.where(causal, s, -1e30)
        p = jnp.exp(s - log)
        t = p * dot_nt(gh, v[:width, :])
        row = jnp.sum(t, axis=1, keepdims=True)
        low = (t - p * row).astype(BF16)
        ps[part, :width] = p.astype(BF16)
        ds[part, :width] = low
        dq = jnp.where(mine, dot_nn(low, k[:width, :]), dq)
    key = dot_tn(ds[:, :width], ps[:, SEQ_LEN:])
    val = dot_tn(ps[:, :width], ds[:, SEQ_LEN : SEQ_LEN + 256])
    if i == 3:
        dk[...] = key
        dv[...] = val
    else:
        dk[:width, :] += key
        dv[:width, :] += val
    cos, sin = tables(tab, rows)
    dh[rows, :256] = turn(dq * HD**-0.5, cos, -sin).astype(BF16)


def keys_back(tab, dh, dk, dv):
    @pl.loop(0, 4)
    def _(i):
        rows = rows_of(i)
        cos, sin = tables(tab, rows)
        dh[rows, 256:512] = turn(dk[rows, :], cos, -sin).astype(BF16)
        dh[rows, 512:768] = dv[rows, :].astype(BF16)


def branch_out(i, a, wb, o):
    rows = rows_of(i)
    o[rows, :] = dot_nn(a[rows, :], wb[...]).astype(BF16)


def branch_back(i, g, wb, dh):
    rows = rows_of(i)
    back = dot_nt(g[rows, :], wb[...])
    dh[rows, :256] = back[:, :256].astype(BF16)
    dh[rows, 768:] = (back[:, 256:] * dh[rows, 768:].astype(F32)).astype(BF16)


def columns_of(m):
    return pl.ds(pl.multiple_of(m * 256, 256), 256)


def grad_wb(m, a, g, wb):
    cols = columns_of(m)
    wb[:, cols] = dot_tn(a[...], g[:, cols]).astype(BF16)


def normed_back(i, dh, wa, out):
    rows = rows_of(i)
    out[rows, :] = dot_nt(dh[rows, :], wa[...]).astype(BF16)


def grad_wa(m, n, dh, wa):
    cols = columns_of(m)
    wa[cols, :] = dot_tn(n[:, cols], dh[...]).astype(BF16)


def grad_bias(dh, put):
    total = jnp.sum(dh[0:RB, :].astype(F32), axis=0, keepdims=True)
    for i in range(1, 4):
        total = total + jnp.sum(dh[i * RB : (i + 1) * RB, :].astype(F32), axis=0, keepdims=True)
    for j in range(WA // 128):
        put(j, total[:, j * 128 : (j + 1) * 128])


def row_block(ref):
    return lambda i: ref.at[pl.ds(pl.multiple_of(i * TOK, TOK), TOK)]


def row_half(ref):
    return lambda i, h: ref.at[pl.ds(pl.multiple_of(i * TOK + h * (TOK // 2), TOK // 2), TOK // 2)]


def col_block(ref):
    return lambda i: ref.at[:, pl.ds(pl.multiple_of(i * 128, 128), 128)]


def col_half(ref):
    return lambda i, h: ref.at[pl.ds(h * (WB // 2), WB // 2), pl.ds(pl.multiple_of(i * 128, 128), 128)]


def sixteen_rows(i):
    return pl.ds(pl.multiple_of(i * 16, 16), 16)


def load_rows(src, dst, sem):
    copies = [pltpu.make_async_copy(src.at[pl.ds(j * 64, 64)], dst.at[j], sem.at[j]) for j in range(2)]
    for copy in copies:
        copy.start()
    return copies


def loaded(ref, i):
    return ref[lax.div(i, 4), pl.ds(pl.multiple_of(lax.rem(i, 4) * 16, 16), 16), :].astype(F32)


def block_kernel(x_ref, cot_ref, gain_ref, shift_ref, dense_b, down_b, qkv_ref, up_ref, dense_ref, down_ref, qkv_b, up_b, tab_ref,
                 out_ref, ig_ref, vec_out, dqkv_out, dup_out, ddense_out, ddown_out, db_out, xhats,
                 n, g, wa, wb, vecs, bias, o, q, k, v, a, dh, lse, dk, dv, tab,
                 sib_a, sib_b, far_a, near_a, pair_a, far_b, near_b, pair_b, far_o, near_o, pair_o, far_n, near_n, pair_n,
                 part, v1, v2, dbs, ssem, rsem, v0s, v0r, v1s, v1r, v2s, v2r, dss, dsr, lsem):
    f, t = lax.axis_index("fsdp"), lax.axis_index("tp")
    tp, fs = Group("tp"), Group("fsdp")
    wa_own, wb_own = row_block(wa)(f), col_block(wb)(f)
    vec_slot = col_block(vecs)
    own = [pltpu.make_async_copy(x_ref, row_block(o)(t), lsem.at[0])]
    for j in range(3):
        own.append(pltpu.make_async_copy(qkv_ref.at[j], wa_own.at[:, pl.ds(j * 256, 256)], lsem.at[1 + j]))
    own += [
        pltpu.make_async_copy(up_ref, wa_own.at[:, pl.ds(768, 1024)], lsem.at[4]),
        pltpu.make_async_copy(dense_ref, wb_own.at[pl.ds(0, 256)], lsem.at[5]),
        pltpu.make_async_copy(down_ref, wb_own.at[pl.ds(256, 1024)], lsem.at[6]),
        pltpu.make_async_copy(cot_ref, row_block(g)(t), lsem.at[7]),
        pltpu.make_async_copy(tab_ref, tab, lsem.at[8]),
    ]
    for copy in own:
        copy.start()
    f32_row = lambda ref: ref[...].astype(F32).reshape(1, ref.shape[0])
    rows = [f32_row(gain_ref), f32_row(shift_ref), f32_row(dense_b) + f32_row(down_b), jnp.zeros((5, 128), F32)]
    vecs[:, pl.ds(pl.multiple_of(f * 128, 128), 128)] = jnp.concatenate(rows, axis=0)
    for j in range(3):
        bias[0:1, j * 256 : (j + 1) * 256] = qkv_b[j : j + 1, :].astype(F32)
    bias[0:1, 768:] = f32_row(up_b)
    ga = Gather(fs, row_block(wa), row_half(wa), ssem.at[0], rsem.at[0], sibling=True)
    gb = Gather(fs, col_block(wb), col_half(wb), ssem.at[1], rsem.at[1], sibling=True)
    gn = Gather(tp, row_block(o), row_half(o), ssem.at[2], rsem.at[2])
    gg = Gather(tp, row_block(g), row_half(g), ssem.at[3], rsem.at[3])
    so = Scatter(tp, row_block(o), row_half(o), far_o, near_o, pair_o, ssem.at[4], rsem.at[4], 16)
    sn = Scatter(tp, row_block(g), row_half(g), far_n, near_n, pair_n, ssem.at[5], rsem.at[5], 16)
    sa = Scatter(fs, row_block(wa), row_half(wa), far_a, near_a, pair_a, ssem.at[6], rsem.at[6], 16, sib_a)
    sb = Scatter(fs, col_block(wb), col_half(wb), far_b, near_b, pair_b, ssem.at[7], rsem.at[7], 128, sib_b)

    def normalize(r, k):
        block = r * 4 + k
        parked = (near_o if r is tp.r else near_n).at[lax.div(k, 2), lax.rem(k, 2)]

        @pl.loop(0, 2)
        def _(i):
            rows = pl.ds(pl.multiple_of(block * TOK + i * 64, 64), 64)
            xf = o[rows, :].astype(F32)
            centered = xf - jnp.mean(xf, axis=-1, keepdims=True)
            variance = jnp.mean(centered * centered, axis=-1, keepdims=True)
            xhat = centered * lax.rsqrt(variance + EPS)
            n[rows, :] = (xhat * vecs[0:1, :] + vecs[1:2, :]).astype(BF16)
            parked[pl.ds(pl.multiple_of(i * 64, 64), 64), :] = xhat.astype(BF16)

    greet(all_peers(f, t))
    own[0].wait()
    gn.ring(0)
    for d in range(1, 16):
        remote(vec_slot(f), vec_slot(f), v0s.at[d], v0r.at[d], (lax.rem(f + d, 16), t)).start()
    gn.pair_send()
    for copy in own[1:5]:
        copy.wait()
    ga.ring(0)
    for copy in own[5:]:
        copy.wait()
    gn.forward(0)
    for d in range(1, 16):
        source = lax.rem(f + 16 - d, 16)
        remote(vec_slot(source), vec_slot(source), v0s.at[d], v0r.at[d], (source, t)).wait_recv()
    normalize(tp.r, tp.k)
    ga.forward(0)
    gb.ring(0)
    gn.pair_recv()
    ga.pair_send()
    ga.near(0)
    normalize(tp.other, tp.k)
    gn.near(0)
    normalize(tp.r, tp.down)
    normalize(tp.r, tp.up)
    gb.forward(0)
    ga.pair_recv()
    gb.pair_send()
    gg.pair_send()
    gn.forward(1)
    gn.far(0)
    gg.ring(0)
    part[...] = jnp.zeros_like(part)

    @pl.loop(0, TOK // 16)
    def _(i):
        cot = g[pl.ds(pl.multiple_of(t * TOK + i * 16, 16), 16), :].astype(F32)
        part[16:24, :] += cot[:8] + cot[8:]

    normalize(tp.r, tp.far)
    ga.far(0)
    ga.forward(1)
    gn.near(1)
    normalize(tp.other, tp.down)
    normalize(tp.other, tp.up)
    gb.near(0)
    gb.pair_recv()
    ga.near(1)
    gn.far(1)
    normalize(tp.other, tp.far)
    keep = [pltpu.make_async_copy(ref, xhats.at[i], lsem.at[9 + i]) for i, ref in enumerate((near_o, near_n))]
    for copy in keep:
        copy.start()
    ga.far(1)
    ga.finish()

    @pl.loop(0, 4)
    def _(i):
        project(i, n, wa, bias, tab, q, k, v, a, dh)

        @pl.when(i == 0)
        def _():
            gg.forward(0)
            gb.far(0)
            gb.forward(1)

        @pl.when(i == 1)
        def _():
            gg.pair_recv()

        @pl.when(i == 2)
        def _():
            gb.near(1)

    gn.sent()
    attend(0, q, k, v, a, lse)
    attend(1, q, k, v, a, lse)
    gg.near(0)
    gb.far(1)
    attend(2, q, k, v, a, lse)
    attend(3, q, k, v, a, lse)
    gb.finish()
    side = lax.div(tp.far, 2)
    halves = (tp.other * 2 + side, tp.r * 2 + side, tp.other * 2 + 1 - side, tp.r * 2 + 1 - side)
    for copy in keep:
        copy.wait()

    @pl.loop(0, 4)
    def _(i):
        branch_out(pick(i, halves), a, wb, o)

        @pl.when(i == 0)
        def _():
            gg.forward(1)

    gg.far(0)

    @pl.loop(0, 4)
    def _(i):
        @pl.when(i == 2)
        def _():
            gg.near(1)
            gg.far(1)
            so.far(0)
            so.far(1)

        branch_back(jnp.where(i < 2, tp.r * 2 + i, tp.other * 2 + i - 2), g, wb, dh)

    gg.finish()
    so.free(0)

    @pl.loop(0, 8)
    def _(s):
        grad_wb(sb.chip(s), a, g, wb)
        sb.sib_copy(s).start()

        @pl.when(s > 1)
        def _():
            sb.sib_add(s - 2)

        @pl.when(s == 2)
        def _():
            sb.far(0)

        @pl.when(s == 3)
        def _():
            sb.far(1)

        @pl.when(s == 4)
        def _():
            so.relay(0)
            so.free(1)

        @pl.when(s == 5)
        def _():
            sb.free(0)

    sb.sib_add(6)
    sb.sib_add(7)
    sb.free(1)
    so.relay(1)
    for i in (3, 2, 1, 0):
        attend_back(i, q, k, v, lse, tab, dh, dk, dv, a, g)
        if i == 3:
            sb.relay(0)
        if i == 2:
            sb.relay(1)

    def fetch(j):
        turn_, sem = lax.rem(j, 2), lax.rem(j, 2) * 4
        place = turn_ * 2 * RB
        src = xhats.at[1 - turn_, jnp.where(j < 2, side, 1 - side)]
        copies = []
        for half in range(2):
            for i in range(2):
                dst = a.at[pl.ds(pl.multiple_of(place + half * RB + i * TOK, TOK), TOK), pl.ds(0, 1024)]
                piece_in = src.at[i, :, pl.ds(half * 1024, 1024)]
                copies.append(pltpu.make_async_copy(piece_in, dst, lsem.at[29 + sem + half * 2 + i]))
        return copies

    def norm_sums(j):
        place, first = lax.rem(j, 2) * 2 * RB, pick(j, halves) * RB

        @pl.loop(0, RB // 64)
        def _(i):
            rows = pl.ds(pl.multiple_of(first + i * 64, 64), 64)
            for half in range(2):
                cols = slice(half * 1024, half * 1024 + 1024)
                grad = g[rows, cols].astype(F32)
                xhat = a[pl.ds(pl.multiple_of(place + half * RB + i * 64, 64), 64), 0:1024].astype(F32)
                part[0:8, cols] += jnp.sum((grad * xhat).reshape(8, 8, 1024), axis=0)
                part[8:16, cols] += jnp.sum(grad.reshape(8, 8, 1024), axis=0)

    for j in range(2):
        for copy in fetch(jnp.int32(j)):
            copy.start()
    keys_back(tab, dh, dk, dv)

    @pl.loop(0, 4)
    def _(j):
        normed_back(pick(j, halves), dh, wa, g)

        @pl.when(j == 0)
        def _():
            sn.far(0)

        @pl.when(j == 1)
        def _():
            sn.far(1)

        for copy in fetch(j):
            copy.wait()
        norm_sums(j)

        @pl.when(j < 2)
        def _():
            for copy in fetch(j + 2):
                copy.start()

        @pl.when(j == 1)
        def _():
            so.pair()
            sb.pair()

    sn.free(0)
    for row in range(3):
        part[24 + row : 25 + row, :] = jnp.sum(part[row * 8 : row * 8 + 8, :], axis=0, keepdims=True)
    piece = lambda i: part.at[pl.ds(24, 8), pl.ds(pl.multiple_of(i * 128, 128), 128)]
    for d in range(1, 16):
        to = lax.rem(f + d, 16)
        remote(piece(to), v1.at[f], v1s.at[d], v1r.at[d], (to, t)).start()
    v1[f] = part[24:, pl.ds(pl.multiple_of(f * 128, 128), 128)]


    @pl.loop(0, 8)
    def _(s):
        grad_wa(sa.chip(s), n, dh, wa)
        sa.sib_copy(s).start()

        @pl.when(s > 1)
        def _():
            sa.sib_add(s - 2)

        @pl.when(s == 2)
        def _():
            sa.far(0)

        @pl.when(s == 3)
        def _():
            sa.far(1)
            sn.relay(0)
            sn.free(1)

        @pl.when(s == 5)
        def _():
            sa.free(0)

    sa.sib_add(6)
    sa.sib_add(7)
    sa.free(1)

    def put(j, row):
        dbs[f, j : j + 1, :] = row

    grad_bias(dh, put)
    dbs[f, WA // 128 :, :] = jnp.zeros((16 - WA // 128, 128), F32)
    for d in range(1, 16):
        remote(dbs.at[f], dbs.at[f], dss.at[d], dsr.at[d], (lax.rem(f + d, 16), t)).start()
    for d in range(1, 16):
        source = lax.rem(f + 16 - d, 16)
        remote(piece(source), v1.at[source], v1s.at[d], v1r.at[d], (source, t)).wait_recv()
    v2[t] = jnp.sum(v1[...], axis=0)
    for d in range(1, 8):
        remote(v2.at[t], v2.at[t], v2s.at[d], v2r.at[d], (f, lax.rem(t + d, 8))).start()
    sn.relay(1)
    sa.relay(0)
    out_refs = so.last()
    rows_in = load_rows(x_ref, far_o.at[1], lsem.at[pl.ds(27, 2)])
    for copy in rows_in:
        copy.wait()

    @pl.loop(0, TOK // 16)
    def _(i):
        rows = sixteen_rows(i)
        total = loaded(far_o.at[1], i) + vecs[2:3, :]
        for ref in out_refs:
            total = total + ref[rows, :].astype(F32)
        pair_o[rows, :] = total.astype(BF16)

    results = [pltpu.make_async_copy(pair_o, out_ref, lsem.at[14])]
    results[0].start()
    cots = load_rows(cot_ref, far_o.at[0], lsem.at[pl.ds(25, 2)])

    sa.relay(1)
    sb_refs = sb.last()
    dense_sum, down_sum = dk.at[pl.ds(0, 256), pl.ds(128, 128)], dk.at[:, pl.ds(0, 128)]
    add_rows(dense_sum, [ref.at[pl.ds(0, 256)] for ref in sb_refs], 128)
    add_rows(down_sum, [ref.at[pl.ds(256, 1024)] for ref in sb_refs], 128)
    results.append(pltpu.make_async_copy(dense_sum, ddense_out, lsem.at[15]))
    results.append(pltpu.make_async_copy(down_sum, ddown_out, lsem.at[16]))
    results[1].start()
    results[2].start()
    sn.pair()
    sa.pair()
    for d in range(1, 16):
        source = lax.rem(f + 16 - d, 16)
        remote(dbs.at[source], dbs.at[source], dss.at[d], dsr.at[d], (source, t)).wait_recv()
    db_out[...] = jnp.sum(dbs[...], axis=0)
    for d in range(1, 8):
        source = lax.rem(t + 8 - d, 8)
        remote(v2.at[source], v2.at[source], v2s.at[d], v2r.at[d], (f, source)).wait_recv()
    vec_out[...] = jnp.sum(v2[...], axis=0)
    for copy in cots:
        copy.wait()
    n_refs = sn.last()

    @pl.loop(0, 2)
    def _(i):
        rows = pl.ds(pl.multiple_of(i * 64, 64), 64)
        xf = far_o[1, i].astype(F32)
        centered = xf - jnp.mean(xf, axis=-1, keepdims=True)
        inv = lax.rsqrt(jnp.mean(centered * centered, axis=-1, keepdims=True) + EPS)
        xhat = centered * inv
        total = n_refs[0][rows, :].astype(F32)
        for ref in n_refs[1:]:
            total = total + ref[rows, :].astype(F32)
        e = total * vecs[0:1, :]
        back = (e - jnp.mean(e, axis=-1, keepdims=True) - xhat * jnp.mean(e * xhat, axis=-1, keepdims=True)) * inv
        pair_n[rows, :] = (far_o[0, i].astype(F32) + back).astype(BF16)

    results.append(pltpu.make_async_copy(pair_n, ig_ref, lsem.at[17]))
    results[3].start()
    sa_refs = sa.last()
    for j in range(7):
        here = dv.at[pl.ds(j * TOK, TOK)]
        add_rows(here, [ref.at[:, pl.ds(j * 256, 256)] for ref in sa_refs], TOK)
        there = dqkv_out.at[j] if j < 3 else dup_out.at[:, pl.ds((j - 3) * 256, 256)]
        results.append(pltpu.make_async_copy(here, there, lsem.at[18 + j]))
        results[-1].start()
    for copy in results:
        copy.wait()
    for op in (so, sn, sa, sb):
        op.sent()
    for d in range(1, 16):
        to = lax.rem(f + d, 16)
        remote(vec_slot(f), vec_slot(f), v0s.at[d], v0r.at[d], (to, t)).wait_send()
        remote(dbs.at[f], dbs.at[f], dss.at[d], dsr.at[d], (to, t)).wait_send()
        remote(piece(to), v1.at[f], v1s.at[d], v1r.at[d], (to, t)).wait_send()
    for d in range(1, 8):
        remote(v2.at[t], v2.at[t], v2s.at[d], v2r.at[d], (f, lax.rem(t + d, 8))).wait_send()


def run_block(*operands):
    def bufs(full, half):
        return [pltpu.VMEM((2, 2) + half, BF16), pltpu.VMEM((2, 2) + full, BF16), pltpu.VMEM(full, BF16)]

    dma = pltpu.SemaphoreType.DMA
    sds = jax.ShapeDtypeStruct
    return pl.pallas_call(
        block_kernel,
        out_shape=(
            sds((TOK, D), BF16),
            sds((TOK, D), BF16),
            sds((8, 128), F32),
            sds((3, TOK, 256), F32),
            sds((TOK, 1024), F32),
            sds((256, 128), F32),
            sds((1024, 128), F32),
            sds((16, 128), F32),
            sds((2, 2, 2, TOK, D), BF16),
        ),
        in_specs=[ANY, ANY, VMEM, VMEM, VMEM, VMEM, ANY, ANY, ANY, ANY, VMEM, VMEM, ANY],
        out_specs=(ANY, ANY, VMEM, ANY, ANY, ANY, ANY, VMEM, ANY),
        scratch_shapes=[
            pltpu.VMEM((SEQ_LEN, D), BF16),
            pltpu.VMEM((SEQ_LEN, D), BF16),
            pltpu.VMEM((D, WA), BF16),
            pltpu.VMEM((WB, D), BF16),
            pltpu.VMEM((8, D), F32),
            pltpu.VMEM((1, WA), F32),
            pltpu.VMEM((SEQ_LEN, D), BF16),
            pltpu.VMEM((SEQ_LEN, 256), BF16),
            pltpu.VMEM((SEQ_LEN, 256), BF16),
            pltpu.VMEM((SEQ_LEN, 256), BF16),
            pltpu.VMEM((SEQ_LEN, WB), BF16),
            pltpu.VMEM((SEQ_LEN, WA), BF16),
            pltpu.VMEM((SEQ_LEN, 128), F32),
            pltpu.VMEM((SEQ_LEN, 256), F32),
            pltpu.VMEM((SEQ_LEN, 256), F32),
            pltpu.VMEM((2, SEQ_LEN, 128), F32),
            pltpu.VMEM((8, TOK, WA), BF16),
            pltpu.VMEM((8, WB, 128), BF16),
            *bufs((TOK, WA), (TOK // 2, WA)),
            *bufs((WB, 128), (WB // 2, 128)),
            *bufs((TOK, D), (TOK // 2, D)),
            *bufs((TOK, D), (TOK // 2, D)),
            pltpu.VMEM((32, D), F32),
            pltpu.VMEM((16, 8, 128), F32),
            pltpu.VMEM((8, 8, 128), F32),
            pltpu.VMEM((16, 16, 128), F32),
            dma((8, 21)), dma((8, 21)),
            dma((16,)), dma((16,)), dma((16,)), dma((16,)), dma((8,)), dma((8,)), dma((16,)), dma((16,)), dma((37,)),
        ],
        compiler_params=pltpu.CompilerParams(collective_id=0, has_side_effects=True, vmem_limit_bytes=64 * 2**20 - 2**18),
        name="block_all",
    )(*operands)


def give_kernel(out_in, ig_in, dqkv_in, dup_in, ddense_in, ddown_in, vec, db,
                out, ig, gain, shift, dqkv, qkv_b, ddense, dense_b, dup, up_b, ddown, down_b, sem):
    pairs = [(out_in, out), (ig_in, ig), (dqkv_in, dqkv), (dup_in, dup), (ddense_in, ddense), (ddown_in, ddown)]
    copies = [pltpu.make_async_copy(src, dst, sem.at[i]) for i, (src, dst) in enumerate(pairs)]
    for copy in copies:
        copy.start()
    gain[...] = vec[0, :]
    shift[...] = vec[1, :]
    dense_b[...] = vec[2, :]
    down_b[...] = vec[2, :]
    for j in range(6):
        qkv_b[j // 2 : j // 2 + 1, (j % 2) * 128 : (j % 2) * 128 + 128] = db[j : j + 1, :]
    for j in range(8):
        up_b[pl.ds(j * 128, 128)] = db[6 + j, :]
    for copy in copies:
        copy.wait()


def give(*results):
    sds = jax.ShapeDtypeStruct
    return pl.pallas_call(
        give_kernel,
        out_shape=(
            sds((TOK, D), BF16),
            sds((TOK, D), BF16),
            sds((128,), F32),
            sds((128,), F32),
            sds((3, TOK, 256), F32),
            sds((3, 256), F32),
            sds((256, 128), F32),
            sds((128,), F32),
            sds((TOK, 1024), F32),
            sds((1024,), F32),
            sds((1024, 128), F32),
            sds((128,), F32),
        ),
        in_specs=[VMEM] * 8,
        out_specs=(ANY, ANY, VMEM, VMEM, ANY, VMEM, ANY, VMEM, ANY, VMEM, ANY, VMEM),
        scratch_shapes=[pltpu.SemaphoreType.DMA((6,))],
        compiler_params=pltpu.CompilerParams(vmem_limit_bytes=60 * 2**20),
        name="give",
    )(*results)


def on_device(
    block_input, norm_gain, norm_bias, qkv_weight, qkv_bias, dense_weight, dense_bias, up_weight, up_bias,
    down_weight, down_bias, cotangent,
):
    out, ig, vec, dqkv, dup, ddense, ddown, db, _ = run_block(
        block_input, cotangent, norm_gain, norm_bias, dense_bias, down_bias, jnp.transpose(qkv_weight, (1, 0, 2)),
        up_weight, dense_weight, down_weight, qkv_bias, up_bias, jnp.asarray(rotary_rows()),
    )
    results = list(give(out, ig, dqkv, dup, ddense, ddown, vec, db))
    results[4] = jnp.transpose(results[4], (1, 0, 2))
    return tuple(results)


def solution(mesh):
    in_specs = (
        P(("fsdp", "tp"), None),
        P("fsdp"),
        P("fsdp"),
        P("fsdp", None, "tp"),
        P(None, "tp"),
        P("tp", "fsdp"),
        P("fsdp"),
        P("fsdp", "tp"),
        P("tp"),
        P("tp", "fsdp"),
        P("fsdp"),
        P(("fsdp", "tp"), None),
    )
    out_specs = (
        P(("fsdp", "tp"), None),
        P(("fsdp", "tp"), None),
        P("fsdp"),
        P("fsdp"),
        P("fsdp", None, "tp"),
        P(None, "tp"),
        P("tp", "fsdp"),
        P("fsdp"),
        P("fsdp", "tp"),
        P("tp"),
        P("tp", "fsdp"),
        P("fsdp"),
    )
    return jax.shard_map(
        on_device, mesh=mesh, in_specs=in_specs, out_specs=out_specs, check_vma=False
    )
```

```python
import jax
import jax.numpy as jnp
import numpy as np
from jax import lax
from jax.experimental import pallas as pl
from jax.experimental.pallas import tpu as pltpu
from jax.sharding import PartitionSpec as P

HD = 64
ROT = 32
SEQ_LEN = 1024
EPS = 1e-05
D = 2048
TOK = 128
WA = 1792
WB = 1280
GELU = 0.7978845608028654
F32 = jnp.float32
BF16 = jnp.bfloat16
MESH = pl.DeviceIdType.MESH
ANY = pl.BlockSpec(memory_space=pl.ANY)
VMEM = pl.BlockSpec(memory_space=pltpu.VMEM)


def place():
    f = lax.axis_index("fsdp")
    t = lax.axis_index("tp")
    return f, t, lax.div(f, 4), lax.rem(lax.div(f, 2), 2), lax.rem(f, 2), lax.div(t, 4), lax.rem(t, 4)


def greet(peers):
    barrier = pltpu.get_barrier_semaphore()
    for peer in peers:
        pl.semaphore_signal(barrier, inc=1, device_id=peer, device_id_type=MESH)
    pl.semaphore_wait(barrier, len(peers))


def all_peers(f, t):
    peers = [(lax.rem(f + d, 16), t) for d in range(1, 16)]
    return peers + [(f, lax.rem(t + d, 8)) for d in range(1, 8)]


def remote(src, dst, ssem, rsem, to):
    return pltpu.make_async_remote_copy(
        src_ref=src, dst_ref=dst, send_sem=ssem, recv_sem=rsem, device_id=to, device_id_type=MESH
    )


class Group:
    def __init__(self, axis):
        f, t, z, yl, c, yh, x = place()
        self.axis = axis
        if axis == "tp":
            self.k, self.r, self.c = x, yh, 0
            self.dev = lambda r, k: (f, r * 4 + k)
        else:
            self.k, self.r, self.c = z, yl, c
            self.dev = lambda r, k: ((k * 2 + r) * 2 + c, t)
            self.sib = ((z * 2 + yl) * 2 + 1 - c, t)
        self.up, self.down, self.far = lax.rem(self.k + 1, 4), lax.rem(self.k + 3, 4), lax.rem(self.k + 2, 4)
        self.other = 1 - self.r

    def index(self, r, k, c=None):
        if self.axis == "tp":
            return r * 4 + k
        return (k * 2 + r) * 2 + (self.c if c is None else c)


class Mover:
    def __init__(self, group, ssem, rsem):
        self.g, self.ssem, self.rsem, self.plan, self.lands = group, ssem, rsem, {}, {}

    def send(self, *numbers):
        for n in numbers:
            src, dst, to = self.plan[n]
            remote(src, dst, self.ssem.at[n], self.rsem.at[n], to).start()

    def recv(self, *numbers):
        for n in numbers:
            land = self.lands[n]
            remote(land, land, self.ssem.at[n], self.rsem.at[n], self.plan[n][2]).wait_recv()

    def sent(self):
        for n, (src, dst, to) in self.plan.items():
            remote(src, dst, self.ssem.at[n], self.rsem.at[n], to).wait_send()


class Gather(Mover):
    def __init__(self, group, block, half, ssem, rsem, sibling=False):
        super().__init__(group, ssem, rsem)
        g = group
        self.sibling = sibling

        def add(n, src, land, to):
            self.plan[n], self.lands[n] = (src, src, to), land

        add(0, block(g.index(g.r, g.k)), block(g.index(g.other, g.k)), g.dev(g.other, g.k))
        for row, r in enumerate((g.r, g.other)):
            up, down = g.dev(g.r, g.up), g.dev(g.r, g.down)
            here = g.index(r, g.k)
            above, below, far = g.index(r, g.up), g.index(r, g.down), g.index(r, g.far)
            n = 1 + 4 * row
            add(n, half(here, 0), half(below, 0), up)
            add(n + 1, half(here, 1), half(above, 1), down)
            add(n + 2, half(here, 1), half(below, 1), up)
            add(n + 3, half(here, 0), half(above, 0), down)
            add(9 + 2 * row, half(below, 0), half(far, 0), up)
            add(10 + 2 * row, half(above, 1), half(far, 1), down)
        if sibling:
            for row, r in enumerate((g.r, g.other)):
                for j, k in enumerate((g.k, g.down, g.up, g.far)):
                    add(13 + 4 * row + j, block(g.index(r, k)), block(g.index(r, k, 1 - g.c)), g.sib)

    def pass_on(self, *numbers):
        if self.sibling:
            self.send(*numbers)

    def ring(self, row):
        n = 1 + 4 * row
        self.send(n, n + 1, n + 2, n + 3)
        self.pass_on(13 + 4 * row)

    def pair_send(self):
        self.send(0)

    def pair_recv(self):
        self.recv(0)
        self.ring(1)

    def forward(self, row):
        n = 1 + 4 * row
        self.recv(n)
        self.send(9 + 2 * row)
        self.recv(n + 1)
        self.send(10 + 2 * row)

    def near(self, row):
        n = 1 + 4 * row
        self.recv(n + 2, n + 3)
        self.pass_on(14 + 4 * row, 15 + 4 * row)

    def far(self, row):
        self.recv(9 + 2 * row, 10 + 2 * row)
        self.pass_on(16 + 4 * row)

    def finish(self):
        if self.sibling:
            self.recv(*range(13, 21))
        self.sent()


def pick(i, values):
    out = values[0]
    for j, value in enumerate(values[1:], 1):
        out = jnp.where(i == j, value, out)
    return out


def add_rows(out, ins, chunk):
    @pl.loop(0, out.shape[0] // chunk)
    def _(i):
        rows = pl.ds(pl.multiple_of(i * chunk, chunk), chunk)
        total = ins[0][rows, :].astype(F32)
        for ref in ins[1:]:
            total = total + ref[rows, :].astype(F32)
        out[rows, :] = total.astype(out.dtype)


class Scatter(Mover):
    def __init__(self, group, block, half, far, near, pair, ssem, rsem, chunk, sib=None):
        super().__init__(group, ssem, rsem)
        g = group
        self.block, self.half, self.chunk = block, half, chunk
        self.far_ref, self.near_ref, self.pair_ref, self.sib_ref = far, near, pair, sib
        self.rows = (g.other, g.r)
        self.order = [(g.other, g.far), (g.r, g.far), (g.other, g.up), (g.other, g.down)]
        self.order += [(g.r, g.up), (g.r, g.down), (g.other, g.k), (g.r, g.k)]
        size = near.shape[2] // 2

        def add(n, src, dst, to):
            self.plan[n], self.lands[n] = (src, dst, to), dst

        for row, r in enumerate(self.rows):
            n = 6 * row
            up, down = g.dev(g.r, g.up), g.dev(g.r, g.down)
            above, below, far_at = g.index(r, g.up), g.index(r, g.down), g.index(r, g.far)
            add(n, half(far_at, 0), far.at[row, 0], up)
            add(n + 1, half(far_at, 1), far.at[row, 1], down)
            add(n + 2, half(above, 1), near.at[row, 0, pl.ds(size, size)], up)
            add(n + 3, half(below, 0), near.at[row, 1, pl.ds(0, size)], down)
            add(n + 4, half(above, 0), near.at[row, 0, pl.ds(0, size)], up)
            add(n + 5, half(below, 1), near.at[row, 1, pl.ds(size, size)], down)
        add(12, block(g.index(g.other, g.k)), pair, g.dev(g.other, g.k))
        if sib is not None:
            for s, (r, k) in enumerate(self.order):
                add(13 + s, block(g.index(r, k, 1 - g.c)), sib.at[s], g.sib)

    def chip(self, s):
        return pick(s, [k * 2 + r for r, k in self.order])

    def sib_copy(self, s):
        src, dst = self.block(self.chip(s) * 2 + 1 - self.g.c), self.sib_ref.at[s]
        return remote(src, dst, self.ssem.at[13 + s], self.rsem.at[13 + s], self.g.sib)

    def sib_add(self, s):
        self.sib_copy(s).wait_recv()
        mine = self.block(self.chip(s) * 2 + self.g.c)
        add_rows(mine, [mine, self.sib_ref.at[s]], self.chunk)

    def far(self, row):
        self.send(6 * row, 6 * row + 1)

    def free(self, row):
        self.send(6 * row + 2, 6 * row + 3)

    def relay(self, row):
        for way, k in ((0, self.g.up), (1, self.g.down)):
            n = 6 * row + way
            self.recv(n)
            mine = self.half(self.g.index(self.rows[row], k), way)
            add_rows(mine, [mine, self.far_ref.at[row, way]], self.chunk)
            self.send(n + 4)

    def pair(self):
        self.recv(2, 3, 4, 5)
        mine = self.block(self.g.index(*self.order[6]))
        add_rows(mine, [mine, self.near_ref.at[0, 0], self.near_ref.at[0, 1]], self.chunk)
        self.send(12)

    def last(self):
        self.recv(8, 9, 10, 11, 12)
        return [self.block(self.g.index(*self.order[7])), self.near_ref.at[1, 0], self.near_ref.at[1, 1], self.pair_ref]


def dot_nn(a, b):
    return jnp.dot(a, b, preferred_element_type=F32)


def dot_nt(a, b):
    return lax.dot_general(a, b, (((1,), (1,)), ((), ())), preferred_element_type=F32)


def dot_tn(a, b):
    return lax.dot_general(a, b, (((0,), (0,)), ((), ())), preferred_element_type=F32)


def rotary_rows():
    lane = np.arange(128) % HD
    freqs = (10000.0 ** (-np.arange(ROT // 2) * 2.0 / ROT)).astype(np.float32)
    angle = np.arange(SEQ_LEN, dtype=np.float32)[:, None] * freqs[lane % (ROT // 2)][None, :]
    turned = lane < ROT
    cos = np.where(turned, np.cos(angle), 1.0)
    sin = np.where(turned, np.sin(angle) * np.where(lane < ROT // 2, -1.0, 1.0), 0.0)
    return np.stack([cos, sin]).astype(np.float32)


def turn(values, cos, sin):
    lane = lax.broadcasted_iota(jnp.int32, values.shape, 1)
    first = lax.rem(lane, HD) < ROT // 2
    partner = jnp.where(first, pltpu.roll(values, 240, 1), pltpu.roll(values, 16, 1))
    return values * cos + partner * sin


def tables(tab, rows):
    cos, sin = tab[0, rows, :], tab[1, rows, :]
    return jnp.concatenate([cos, cos], axis=1), jnp.concatenate([sin, sin], axis=1)


def head_lanes(h, rows):
    lane = lax.broadcasted_iota(jnp.int32, (rows, 256), 1)
    return lax.div(lane, HD) == h


RB = 256


def rows_of(i):
    return pl.ds(pl.multiple_of(i * RB, RB), RB)


def project(i, n, wa, bias, tab, q, k, v, a, dh):
    rows = rows_of(i)
    cos, sin = tables(tab, rows)
    joined = dot_nn(n[rows, :], wa[...]) + bias[0:1, :]
    q[rows, :] = (turn(joined[:, :256], cos, sin) * HD**-0.5).astype(BF16)
    k[rows, :] = turn(joined[:, 256:512], cos, sin).astype(BF16)
    v[rows, :] = joined[:, 512:768].astype(BF16)
    z = joined[:, 768:]
    z2 = z * z
    th = jnp.tanh(z * (GELU + (GELU * 0.044715) * z2))
    half = 0.5 + 0.5 * th
    a[rows, 256:] = (z * half).astype(BF16)
    dh[rows, 768:] = (half + (half - half * half) * z * (2 * GELU + (6 * GELU * 0.044715) * z2)).astype(BF16)


def attend(i, q, k, v, a, lse):
    rows, before = slice(i * RB, (i + 1) * RB), i * RB
    qb = q[rows, :]
    causal = lax.broadcasted_iota(jnp.int32, (RB, RB), 1) <= lax.broadcasted_iota(jnp.int32, (RB, RB), 0)
    lane = lax.broadcasted_iota(jnp.int32, (RB, 128), 1)
    context = jnp.zeros((RB, 256), F32)
    logs = jnp.zeros((RB, 128), F32)
    for h in range(4):
        mine = head_lanes(h, RB)
        qh = jnp.where(mine, qb, jnp.zeros_like(qb))
        s1 = jnp.where(causal, dot_nt(qh, k[rows, :]), -1e30)
        top = jnp.max(s1, axis=1, keepdims=True)
        if i:
            s0 = dot_nt(qh, k[:before, :])
            top = jnp.maximum(top, jnp.max(s0, axis=1, keepdims=True))
        p1 = jnp.exp(s1 - top)
        total = jnp.sum(p1, axis=1, keepdims=True)
        out = dot_nn(p1.astype(BF16), v[rows, :])
        if i:
            p0 = jnp.exp(s0 - top)
            total = total + jnp.sum(p0, axis=1, keepdims=True)
            out = out + dot_nn(p0.astype(BF16), v[:before, :])
        context = jnp.where(mine, out / total, context)
        logs = jnp.where(lane == h, top + jnp.log(total), logs)
    a[rows, :256] = context.astype(BF16)
    lse[rows, :] = logs


def attend_back(i, q, k, v, lse, tab, dh, dk, dv, ps, ds):
    rows, width = slice(i * RB, (i + 1) * RB), (i + 1) * RB
    qb, gb = q[rows, :], dh[rows, :256]
    causal = lax.broadcasted_iota(jnp.int32, (RB, RB), 1) <= lax.broadcasted_iota(jnp.int32, (RB, RB), 0)
    dq = jnp.zeros((RB, 256), F32)
    for h in range(4):
        mine = head_lanes(h, RB)
        part = slice(h * RB, (h + 1) * RB)
        qh = jnp.where(mine, qb, jnp.zeros_like(qb))
        gh = jnp.where(mine, gb, jnp.zeros_like(gb))
        ps[part, SEQ_LEN:] = qh
        ds[part, SEQ_LEN : SEQ_LEN + 256] = gh
        log = lse[rows, h : h + 1]
        s = dot_nt(qh, k[:width, :])
        if i:
            s = jnp.concatenate([s[:, : i * RB], jnp.where(causal, s[:, i * RB :], -1e30)], axis=1)
        else:
            s = jnp.where(causal, s, -1e30)
        p = jnp.exp(s - log)
        t = p * dot_nt(gh, v[:width, :])
        row = jnp.sum(t, axis=1, keepdims=True)
        low = (t - p * row).astype(BF16)
        ps[part, :width] = p.astype(BF16)
        ds[part, :width] = low
        dq = jnp.where(mine, dot_nn(low, k[:width, :]), dq)
    key = dot_tn(ds[:, :width], ps[:, SEQ_LEN:])
    val = dot_tn(ps[:, :width], ds[:, SEQ_LEN : SEQ_LEN + 256])
    if i == 3:
        dk[...] = key
        dv[...] = val
    else:
        dk[:width, :] += key
        dv[:width, :] += val
    cos, sin = tables(tab, rows)
    dh[rows, :256] = turn(dq * HD**-0.5, cos, -sin).astype(BF16)


def keys_back(tab, dh, dk, dv):
    @pl.loop(0, 4)
    def _(i):
        rows = rows_of(i)
        cos, sin = tables(tab, rows)
        dh[rows, 256:512] = turn(dk[rows, :], cos, -sin).astype(BF16)
        dh[rows, 512:768] = dv[rows, :].astype(BF16)


def branch_out(i, a, wb, o):
    rows = rows_of(i)
    o[rows, :] = dot_nn(a[rows, :], wb[...]).astype(BF16)


def branch_back(i, g, wb, dh):
    rows = rows_of(i)
    back = dot_nt(g[rows, :], wb[...])
    dh[rows, :256] = back[:, :256].astype(BF16)
    dh[rows, 768:] = (back[:, 256:] * dh[rows, 768:].astype(F32)).astype(BF16)


def columns_of(m):
    return pl.ds(pl.multiple_of(m * 256, 256), 256)


def grad_wb(m, a, g, wb):
    cols = columns_of(m)
    wb[:, cols] = dot_tn(a[...], g[:, cols]).astype(BF16)


def normed_back(i, dh, wa, out):
    rows = rows_of(i)
    out[rows, :] = dot_nt(dh[rows, :], wa[...]).astype(BF16)


def grad_wa(m, n, dh, wa):
    cols = columns_of(m)
    wa[cols, :] = dot_tn(n[:, cols], dh[...]).astype(BF16)


def grad_bias(dh, put):
    total = jnp.sum(dh[0:RB, :].astype(F32), axis=0, keepdims=True)
    for i in range(1, 4):
        total = total + jnp.sum(dh[i * RB : (i + 1) * RB, :].astype(F32), axis=0, keepdims=True)
    for j in range(WA // 128):
        put(j, total[:, j * 128 : (j + 1) * 128])


def row_block(ref):
    return lambda i: ref.at[pl.ds(pl.multiple_of(i * TOK, TOK), TOK)]


def row_half(ref):
    return lambda i, h: ref.at[pl.ds(pl.multiple_of(i * TOK + h * (TOK // 2), TOK // 2), TOK // 2)]


def col_block(ref):
    return lambda i: ref.at[:, pl.ds(pl.multiple_of(i * 128, 128), 128)]


def col_half(ref):
    return lambda i, h: ref.at[pl.ds(h * (WB // 2), WB // 2), pl.ds(pl.multiple_of(i * 128, 128), 128)]


def sixteen_rows(i):
    return pl.ds(pl.multiple_of(i * 16, 16), 16)


def load_rows(src, dst, sem):
    copies = [pltpu.make_async_copy(src.at[pl.ds(j * 64, 64)], dst.at[j], sem.at[j]) for j in range(2)]
    for copy in copies:
        copy.start()
    return copies


def loaded(ref, i):
    return ref[lax.div(i, 4), pl.ds(pl.multiple_of(lax.rem(i, 4) * 16, 16), 16), :].astype(F32)


def block_kernel(x_ref, cot_ref, gain_ref, shift_ref, dense_b, down_b, qkv_ref, up_ref, dense_ref, down_ref, qkv_b, up_b, tab_ref,
                 out_ref, ig_ref, vec_out, dqkv_out, dup_out, ddense_out, ddown_out, db_out, xhats,
                 n, g, wa, wb, vecs, bias, o, q, k, v, a, dh, lse, dk, dv, tab,
                 sib_a, sib_b, far_a, near_a, pair_a, far_b, near_b, pair_b, far_o, near_o, pair_o, far_n, near_n, pair_n,
                 part, v1, v2, dbs, ssem, rsem, v0s, v0r, v1s, v1r, v2s, v2r, dss, dsr, lsem):
    f, t = lax.axis_index("fsdp"), lax.axis_index("tp")
    tp, fs = Group("tp"), Group("fsdp")
    wa_own, wb_own = row_block(wa)(f), col_block(wb)(f)
    vec_slot = col_block(vecs)
    own = [pltpu.make_async_copy(x_ref, row_block(o)(t), lsem.at[0])]
    for j in range(3):
        own.append(pltpu.make_async_copy(qkv_ref.at[j], wa_own.at[:, pl.ds(j * 256, 256)], lsem.at[1 + j]))
    own += [
        pltpu.make_async_copy(up_ref, wa_own.at[:, pl.ds(768, 1024)], lsem.at[4]),
        pltpu.make_async_copy(dense_ref, wb_own.at[pl.ds(0, 256)], lsem.at[5]),
        pltpu.make_async_copy(down_ref, wb_own.at[pl.ds(256, 1024)], lsem.at[6]),
        pltpu.make_async_copy(cot_ref, row_block(g)(t), lsem.at[7]),
        pltpu.make_async_copy(tab_ref, tab, lsem.at[8]),
    ]
    for copy in own:
        copy.start()
    f32_row = lambda ref: ref[...].astype(F32).reshape(1, ref.shape[0])
    rows = [f32_row(gain_ref), f32_row(shift_ref), f32_row(dense_b) + f32_row(down_b), jnp.zeros((5, 128), F32)]
    vecs[:, pl.ds(pl.multiple_of(f * 128, 128), 128)] = jnp.concatenate(rows, axis=0)
    for j in range(3):
        bias[0:1, j * 256 : (j + 1) * 256] = qkv_b[j : j + 1, :].astype(F32)
    bias[0:1, 768:] = f32_row(up_b)
    ga = Gather(fs, row_block(wa), row_half(wa), ssem.at[0], rsem.at[0], sibling=True)
    gb = Gather(fs, col_block(wb), col_half(wb), ssem.at[1], rsem.at[1], sibling=True)
    gn = Gather(tp, row_block(o), row_half(o), ssem.at[2], rsem.at[2])
    gg = Gather(tp, row_block(g), row_half(g), ssem.at[3], rsem.at[3])
    so = Scatter(tp, row_block(o), row_half(o), far_o, near_o, pair_o, ssem.at[4], rsem.at[4], 16)
    sn = Scatter(tp, row_block(g), row_half(g), far_n, near_n, pair_n, ssem.at[5], rsem.at[5], 16)
    sa = Scatter(fs, row_block(wa), row_half(wa), far_a, near_a, pair_a, ssem.at[6], rsem.at[6], 16, sib_a)
    sb = Scatter(fs, col_block(wb), col_half(wb), far_b, near_b, pair_b, ssem.at[7], rsem.at[7], 128, sib_b)

    def normalize(r, k):
        block = r * 4 + k
        parked = (near_o if r is tp.r else near_n).at[lax.div(k, 2), lax.rem(k, 2)]

        @pl.loop(0, 2)
        def _(i):
            rows = pl.ds(pl.multiple_of(block * TOK + i * 64, 64), 64)
            xf = o[rows, :].astype(F32)
            centered = xf - jnp.mean(xf, axis=-1, keepdims=True)
            variance = jnp.mean(centered * centered, axis=-1, keepdims=True)
            xhat = centered * lax.rsqrt(variance + EPS)
            n[rows, :] = (xhat * vecs[0:1, :] + vecs[1:2, :]).astype(BF16)
            parked[pl.ds(pl.multiple_of(i * 64, 64), 64), :] = xhat.astype(BF16)

    greet(all_peers(f, t))
    own[0].wait()
    gn.ring(0)
    for d in range(1, 16):
        remote(vec_slot(f), vec_slot(f), v0s.at[d], v0r.at[d], (lax.rem(f + d, 16), t)).start()
    gn.pair_send()
    for copy in own[1:5]:
        copy.wait()
    ga.ring(0)
    for copy in own[5:]:
        copy.wait()
    gn.forward(0)
    for d in range(1, 16):
        source = lax.rem(f + 16 - d, 16)
        remote(vec_slot(source), vec_slot(source), v0s.at[d], v0r.at[d], (source, t)).wait_recv()
    normalize(tp.r, tp.k)
    ga.forward(0)
    gb.ring(0)
    gn.pair_recv()
    ga.pair_send()
    ga.near(0)
    normalize(tp.other, tp.k)
    gn.near(0)
    normalize(tp.r, tp.down)
    normalize(tp.r, tp.up)
    gb.forward(0)
    ga.pair_recv()
    gb.pair_send()
    gg.pair_send()
    gn.forward(1)
    gn.far(0)
    gg.ring(0)
    part[...] = jnp.zeros_like(part)

    @pl.loop(0, TOK // 16)
    def _(i):
        cot = g[pl.ds(pl.multiple_of(t * TOK + i * 16, 16), 16), :].astype(F32)
        part[16:24, :] += cot[:8] + cot[8:]

    normalize(tp.r, tp.far)
    ga.far(0)
    ga.forward(1)
    gn.near(1)
    normalize(tp.other, tp.down)
    normalize(tp.other, tp.up)
    gb.near(0)
    gb.pair_recv()
    ga.near(1)
    gn.far(1)
    normalize(tp.other, tp.far)
    keep = [pltpu.make_async_copy(ref, xhats.at[i], lsem.at[9 + i]) for i, ref in enumerate((near_o, near_n))]
    for copy in keep:
        copy.start()
    ga.far(1)
    ga.finish()

    @pl.loop(0, 4)
    def _(i):
        project(i, n, wa, bias, tab, q, k, v, a, dh)

        @pl.when(i == 0)
        def _():
            gg.forward(0)
            gb.far(0)
            gb.forward(1)

        @pl.when(i == 1)
        def _():
            gg.pair_recv()

        @pl.when(i == 2)
        def _():
            gb.near(1)

    gn.sent()
    attend(0, q, k, v, a, lse)
    attend(1, q, k, v, a, lse)
    gg.near(0)
    gb.far(1)
    attend(2, q, k, v, a, lse)
    attend(3, q, k, v, a, lse)
    gb.finish()
    side = lax.div(tp.far, 2)
    halves = (tp.other * 2 + side, tp.r * 2 + side, tp.other * 2 + 1 - side, tp.r * 2 + 1 - side)
    for copy in keep:
        copy.wait()

    @pl.loop(0, 4)
    def _(i):
        branch_out(pick(i, halves), a, wb, o)

        @pl.when(i == 0)
        def _():
            gg.forward(1)

    gg.far(0)

    @pl.loop(0, 4)
    def _(i):
        @pl.when(i == 2)
        def _():
            gg.near(1)
            gg.far(1)
            so.far(0)
            so.far(1)

        branch_back(jnp.where(i < 2, tp.r * 2 + i, tp.other * 2 + i - 2), g, wb, dh)

    gg.finish()
    so.free(0)

    @pl.loop(0, 8)
    def _(s):
        grad_wb(sb.chip(s), a, g, wb)
        sb.sib_copy(s).start()

        @pl.when(s > 1)
        def _():
            sb.sib_add(s - 2)

        @pl.when(s == 2)
        def _():
            sb.far(0)

        @pl.when(s == 3)
        def _():
            sb.far(1)

        @pl.when(s == 4)
        def _():
            so.relay(0)
            so.free(1)

        @pl.when(s == 5)
        def _():
            sb.free(0)

    sb.sib_add(6)
    sb.sib_add(7)
    sb.free(1)
    so.relay(1)
    for i in (3, 2, 1, 0):
        attend_back(i, q, k, v, lse, tab, dh, dk, dv, a, g)
        if i == 3:
            sb.relay(0)
        if i == 2:
            sb.relay(1)

    def fetch(j):
        turn_, sem = lax.rem(j, 2), lax.rem(j, 2) * 4
        place = turn_ * 2 * RB
        src = xhats.at[1 - turn_, jnp.where(j < 2, side, 1 - side)]
        copies = []
        for half in range(2):
            for i in range(2):
                dst = a.at[pl.ds(pl.multiple_of(place + half * RB + i * TOK, TOK), TOK), pl.ds(0, 1024)]
                piece_in = src.at[i, :, pl.ds(half * 1024, 1024)]
                copies.append(pltpu.make_async_copy(piece_in, dst, lsem.at[29 + sem + half * 2 + i]))
        return copies

    def norm_sums(j):
        place, first = lax.rem(j, 2) * 2 * RB, pick(j, halves) * RB

        @pl.loop(0, RB // 64)
        def _(i):
            rows = pl.ds(pl.multiple_of(first + i * 64, 64), 64)
            for half in range(2):
                cols = slice(half * 1024, half * 1024 + 1024)
                grad = g[rows, cols].astype(F32)
                xhat = a[pl.ds(pl.multiple_of(place + half * RB + i * 64, 64), 64), 0:1024].astype(F32)
                part[0:8, cols] += jnp.sum((grad * xhat).reshape(8, 8, 1024), axis=0)
                part[8:16, cols] += jnp.sum(grad.reshape(8, 8, 1024), axis=0)

    for j in range(2):
        for copy in fetch(jnp.int32(j)):
            copy.start()
    keys_back(tab, dh, dk, dv)

    @pl.loop(0, 4)
    def _(j):
        normed_back(pick(j, halves), dh, wa, g)

        @pl.when(j == 0)
        def _():
            sn.far(0)

        @pl.when(j == 1)
        def _():
            sn.far(1)

        for copy in fetch(j):
            copy.wait()
        norm_sums(j)

        @pl.when(j < 2)
        def _():
            for copy in fetch(j + 2):
                copy.start()

        @pl.when(j == 1)
        def _():
            so.pair()
            sb.pair()

    sn.free(0)
    for row in range(3):
        part[24 + row : 25 + row, :] = jnp.sum(part[row * 8 : row * 8 + 8, :], axis=0, keepdims=True)
    piece = lambda i: part.at[pl.ds(24, 8), pl.ds(pl.multiple_of(i * 128, 128), 128)]
    for d in range(1, 16):
        to = lax.rem(f + d, 16)
        remote(piece(to), v1.at[f], v1s.at[d], v1r.at[d], (to, t)).start()
    v1[f] = part[24:, pl.ds(pl.multiple_of(f * 128, 128), 128)]


    @pl.loop(0, 8)
    def _(s):
        grad_wa(sa.chip(s), n, dh, wa)
        sa.sib_copy(s).start()

        @pl.when(s > 1)
        def _():
            sa.sib_add(s - 2)

        @pl.when(s == 2)
        def _():
            sa.far(0)

        @pl.when(s == 3)
        def _():
            sa.far(1)
            sn.relay(0)
            sn.free(1)

        @pl.when(s == 5)
        def _():
            sa.free(0)

    sa.sib_add(6)
    sa.sib_add(7)
    sa.free(1)

    def put(j, row):
        dbs[f, j : j + 1, :] = row

    grad_bias(dh, put)
    dbs[f, WA // 128 :, :] = jnp.zeros((16 - WA // 128, 128), F32)
    for d in range(1, 16):
        remote(dbs.at[f], dbs.at[f], dss.at[d], dsr.at[d], (lax.rem(f + d, 16), t)).start()
    for d in range(1, 16):
        source = lax.rem(f + 16 - d, 16)
        remote(piece(source), v1.at[source], v1s.at[d], v1r.at[d], (source, t)).wait_recv()
    v2[t] = jnp.sum(v1[...], axis=0)
    for d in range(1, 8):
        remote(v2.at[t], v2.at[t], v2s.at[d], v2r.at[d], (f, lax.rem(t + d, 8))).start()
    sn.relay(1)
    sa.relay(0)
    out_refs = so.last()
    rows_in = load_rows(x_ref, far_o.at[1], lsem.at[pl.ds(27, 2)])
    for copy in rows_in:
        copy.wait()

    @pl.loop(0, TOK // 16)
    def _(i):
        rows = sixteen_rows(i)
        total = loaded(far_o.at[1], i) + vecs[2:3, :]
        for ref in out_refs:
            total = total + ref[rows, :].astype(F32)
        pair_o[rows, :] = total.astype(BF16)

    results = [pltpu.make_async_copy(pair_o, out_ref, lsem.at[14])]
    results[0].start()
    cots = load_rows(cot_ref, far_o.at[0], lsem.at[pl.ds(25, 2)])

    sa.relay(1)
    sb_refs = sb.last()
    dense_sum, down_sum = dk.at[pl.ds(0, 256), pl.ds(128, 128)], dk.at[:, pl.ds(0, 128)]
    add_rows(dense_sum, [ref.at[pl.ds(0, 256)] for ref in sb_refs], 128)
    add_rows(down_sum, [ref.at[pl.ds(256, 1024)] for ref in sb_refs], 128)
    results.append(pltpu.make_async_copy(dense_sum, ddense_out, lsem.at[15]))
    results.append(pltpu.make_async_copy(down_sum, ddown_out, lsem.at[16]))
    results[1].start()
    results[2].start()
    sn.pair()
    sa.pair()
    for d in range(1, 16):
        source = lax.rem(f + 16 - d, 16)
        remote(dbs.at[source], dbs.at[source], dss.at[d], dsr.at[d], (source, t)).wait_recv()
    db_out[...] = jnp.sum(dbs[...], axis=0)
    for d in range(1, 8):
        source = lax.rem(t + 8 - d, 8)
        remote(v2.at[source], v2.at[source], v2s.at[d], v2r.at[d], (f, source)).wait_recv()
    vec_out[...] = jnp.sum(v2[...], axis=0)
    for copy in cots:
        copy.wait()
    n_refs = sn.last()

    @pl.loop(0, 2)
    def _(i):
        rows = pl.ds(pl.multiple_of(i * 64, 64), 64)
        xf = far_o[1, i].astype(F32)
        centered = xf - jnp.mean(xf, axis=-1, keepdims=True)
        inv = lax.rsqrt(jnp.mean(centered * centered, axis=-1, keepdims=True) + EPS)
        xhat = centered * inv
        total = n_refs[0][rows, :].astype(F32)
        for ref in n_refs[1:]:
            total = total + ref[rows, :].astype(F32)
        e = total * vecs[0:1, :]
        back = (e - jnp.mean(e, axis=-1, keepdims=True) - xhat * jnp.mean(e * xhat, axis=-1, keepdims=True)) * inv
        pair_n[rows, :] = (far_o[0, i].astype(F32) + back).astype(BF16)

    results.append(pltpu.make_async_copy(pair_n, ig_ref, lsem.at[17]))
    results[3].start()
    sa_refs = sa.last()
    for j in range(7):
        here = dv.at[pl.ds(j * TOK, TOK)]
        add_rows(here, [ref.at[:, pl.ds(j * 256, 256)] for ref in sa_refs], TOK)
        there = dqkv_out.at[j] if j < 3 else dup_out.at[:, pl.ds((j - 3) * 256, 256)]
        results.append(pltpu.make_async_copy(here, there, lsem.at[18 + j]))
        results[-1].start()
    for copy in results:
        copy.wait()
    for op in (so, sn, sa, sb):
        op.sent()
    for d in range(1, 16):
        to = lax.rem(f + d, 16)
        remote(vec_slot(f), vec_slot(f), v0s.at[d], v0r.at[d], (to, t)).wait_send()
        remote(dbs.at[f], dbs.at[f], dss.at[d], dsr.at[d], (to, t)).wait_send()
        remote(piece(to), v1.at[f], v1s.at[d], v1r.at[d], (to, t)).wait_send()
    for d in range(1, 8):
        remote(v2.at[t], v2.at[t], v2s.at[d], v2r.at[d], (f, lax.rem(t + d, 8))).wait_send()


def run_block(*operands):
    def bufs(full, half):
        return [pltpu.VMEM((2, 2) + half, BF16), pltpu.VMEM((2, 2) + full, BF16), pltpu.VMEM(full, BF16)]

    dma = pltpu.SemaphoreType.DMA
    sds = jax.ShapeDtypeStruct
    return pl.pallas_call(
        block_kernel,
        out_shape=(
            sds((TOK, D), BF16),
            sds((TOK, D), BF16),
            sds((8, 128), F32),
            sds((3, TOK, 256), F32),
            sds((TOK, 1024), F32),
            sds((256, 128), F32),
            sds((1024, 128), F32),
            sds((16, 128), F32),
            sds((2, 2, 2, TOK, D), BF16),
        ),
        in_specs=[ANY, ANY, VMEM, VMEM, VMEM, VMEM, ANY, ANY, ANY, ANY, VMEM, VMEM, ANY],
        out_specs=(ANY, ANY, VMEM, ANY, ANY, ANY, ANY, VMEM, ANY),
        scratch_shapes=[
            pltpu.VMEM((SEQ_LEN, D), BF16),
            pltpu.VMEM((SEQ_LEN, D), BF16),
            pltpu.VMEM((D, WA), BF16),
            pltpu.VMEM((WB, D), BF16),
            pltpu.VMEM((8, D), F32),
            pltpu.VMEM((1, WA), F32),
            pltpu.VMEM((SEQ_LEN, D), BF16),
            pltpu.VMEM((SEQ_LEN, 256), BF16),
            pltpu.VMEM((SEQ_LEN, 256), BF16),
            pltpu.VMEM((SEQ_LEN, 256), BF16),
            pltpu.VMEM((SEQ_LEN, WB), BF16),
            pltpu.VMEM((SEQ_LEN, WA), BF16),
            pltpu.VMEM((SEQ_LEN, 128), F32),
            pltpu.VMEM((SEQ_LEN, 256), F32),
            pltpu.VMEM((SEQ_LEN, 256), F32),
            pltpu.VMEM((2, SEQ_LEN, 128), F32),
            pltpu.VMEM((8, TOK, WA), BF16),
            pltpu.VMEM((8, WB, 128), BF16),
            *bufs((TOK, WA), (TOK // 2, WA)),
            *bufs((WB, 128), (WB // 2, 128)),
            *bufs((TOK, D), (TOK // 2, D)),
            *bufs((TOK, D), (TOK // 2, D)),
            pltpu.VMEM((32, D), F32),
            pltpu.VMEM((16, 8, 128), F32),
            pltpu.VMEM((8, 8, 128), F32),
            pltpu.VMEM((16, 16, 128), F32),
            dma((8, 21)), dma((8, 21)),
            dma((16,)), dma((16,)), dma((16,)), dma((16,)), dma((8,)), dma((8,)), dma((16,)), dma((16,)), dma((37,)),
        ],
        compiler_params=pltpu.CompilerParams(collective_id=0, has_side_effects=True, vmem_limit_bytes=64 * 2**20 - 2**18),
        name="block_all",
    )(*operands)


def give_kernel(out_in, ig_in, dqkv_in, dup_in, ddense_in, ddown_in, vec, db,
                out, ig, gain, shift, dqkv, qkv_b, ddense, dense_b, dup, up_b, ddown, down_b,
                out_v, ig_v, dqkv_v, dup_v, ddense_v, ddown_v, sem_in, sem_out):
    ways = [(out_in, out_v, out), (ig_in, ig_v, ig), (dup_in, dup_v, dup), (ddown_in, ddown_v, ddown)]
    ways += [(dqkv_in, dqkv_v, dqkv), (ddense_in, ddense_v, ddense)]
    arrive = [pltpu.make_async_copy(src, mid, sem_in.at[i]) for i, (src, mid, _) in enumerate(ways)]
    leave = [pltpu.make_async_copy(mid, dst, sem_out.at[i]) for i, (_, mid, dst) in enumerate(ways)]
    for copy in arrive:
        copy.start()
    for first, second in zip(arrive, leave):
        first.wait()
        second.start()
    gain[...] = vec[0, :]
    shift[...] = vec[1, :]
    dense_b[...] = vec[2, :]
    down_b[...] = vec[2, :]
    for j in range(6):
        qkv_b[j // 2 : j // 2 + 1, (j % 2) * 128 : (j % 2) * 128 + 128] = db[j : j + 1, :]
    for j in range(8):
        up_b[pl.ds(j * 128, 128)] = db[6 + j, :]
    for copy in leave:
        copy.wait()


def give(*results):
    sds = jax.ShapeDtypeStruct
    return pl.pallas_call(
        give_kernel,
        out_shape=(
            sds((TOK, D), BF16),
            sds((TOK, D), BF16),
            sds((128,), F32),
            sds((128,), F32),
            sds((3, TOK, 256), F32),
            sds((3, 256), F32),
            sds((256, 128), F32),
            sds((128,), F32),
            sds((TOK, 1024), F32),
            sds((1024,), F32),
            sds((1024, 128), F32),
            sds((128,), F32),
        ),
        in_specs=[ANY] * 6 + [VMEM] * 2,
        out_specs=(ANY, ANY, VMEM, VMEM, ANY, VMEM, ANY, VMEM, ANY, VMEM, ANY, VMEM),
        scratch_shapes=[
            pltpu.VMEM((TOK, D), BF16),
            pltpu.VMEM((TOK, D), BF16),
            pltpu.VMEM((3, TOK, 256), F32),
            pltpu.VMEM((TOK, 1024), F32),
            pltpu.VMEM((256, 128), F32),
            pltpu.VMEM((1024, 128), F32),
            pltpu.SemaphoreType.DMA((6,)),
            pltpu.SemaphoreType.DMA((6,)),
        ],
        compiler_params=pltpu.CompilerParams(vmem_limit_bytes=60 * 2**20),
        name="give",
    )(*results)


def on_device(
    block_input, norm_gain, norm_bias, qkv_weight, qkv_bias, dense_weight, dense_bias, up_weight, up_bias,
    down_weight, down_bias, cotangent,
):
    out, ig, vec, dqkv, dup, ddense, ddown, db, _ = run_block(
        block_input, cotangent, norm_gain, norm_bias, dense_bias, down_bias, jnp.transpose(qkv_weight, (1, 0, 2)),
        up_weight, dense_weight, down_weight, qkv_bias, up_bias, jnp.asarray(rotary_rows()),
    )
    results = list(give(out, ig, dqkv, dup, ddense, ddown, vec, db))
    results[4] = jnp.transpose(results[4], (1, 0, 2))
    return tuple(results)


def solution(mesh):
    in_specs = (
        P(("fsdp", "tp"), None),
        P("fsdp"),
        P("fsdp"),
        P("fsdp", None, "tp"),
        P(None, "tp"),
        P("tp", "fsdp"),
        P("fsdp"),
        P("fsdp", "tp"),
        P("tp"),
        P("tp", "fsdp"),
        P("fsdp"),
        P(("fsdp", "tp"), None),
    )
    out_specs = (
        P(("fsdp", "tp"), None),
        P(("fsdp", "tp"), None),
        P("fsdp"),
        P("fsdp"),
        P("fsdp", None, "tp"),
        P(None, "tp"),
        P("tp", "fsdp"),
        P("fsdp"),
        P("fsdp", "tp"),
        P("tp"),
        P("tp", "fsdp"),
        P("fsdp"),
    )
    return jax.shard_map(
        on_device, mesh=mesh, in_specs=in_specs, out_specs=out_specs, check_vma=False
    )
```
